32 devices in a mesh: grp: 2 (over y), col: 8 (over z, x), row: 2 (over core).
Axes of the slice: x: 2, y: 2, z: 4, core: 2. Of those that a mesh axis runs over, the one named last changes fastest.
Arguments:
- pair_block: float32 [4, 16, 1152, 128], P('grp', 'row', 'col'), parts along dimension 0, may hold values from -260 to 260
- query_single: bfloat16 [4, 16, 768], P('grp', 'row'), parts along dimension 0, may hold values from -70 to 70
- key_single: bfloat16 [2304, 768], P(('grp', 'col')), parts along dimension 0, may hold values from -70 to 70
- query_chain: int32 [4, 16], P('grp', 'row'), parts along dimension 0, may hold values from 0 to 23
- key_chain: int32 [2304], P(('grp', 'col')), parts along dimension 0, may hold values from 0 to 23, never falling along the last dimension, each value on 1 to 144 neighbouring positions
- query_mask: int32 [4, 16], P('grp', 'row'), parts along dimension 0, may hold values 0 or 1
- key_mask: int32 [2304], P(('grp', 'col')), parts along dimension 0, may hold values 0 or 1
- timestep: int32 [2], P('grp'), parts along dimension 0, may hold values from 0 to 49
- time_table: bfloat16 [50, 768], replicated, may hold values from -6 to 6
- norm_gain: float32 [768], replicated, may hold values from 0.1 to 1.9
- left_proj: bfloat16 [768, 8], replicated, may hold values from -0.21875 to 0.21875
- right_proj: bfloat16 [768, 8], replicated, may hold values from -0.21875 to 0.21875
- outer_proj: bfloat16 [64, 128], replicated, may hold values from -0.75 to 0.75
- bias_proj: float32 [128, 12], replicated, may hold values from -0.75 to 0.75
- chain_weight: float32 [12], replicated, may hold values from -2 to 2
- query_proj: bfloat16 [768, 1536], P(None, 'col'), may hold values from -0.21875 to 0.21875
- kv_proj: bfloat16 [768, 1536], P(None, 'row'), may hold values from -0.21875 to 0.21875
- out_proj: bfloat16 [768, 768], replicated, may hold values from -0.75 to 0.75
Outputs:
- new_pair: float32 [4, 16, 1152, 128], P('grp', 'row', 'col'), parts along dimension 0
- single_update: bfloat16 [4, 16, 768], P('grp', 'row'), parts along dimension 0
The draws below stay inside these ranges and needn't reach their ends.
There are 2 independent parts, one for each index of `grp`. The reference program is written for one: setup_inputs(seed, part) draws one part's arguments, and reference() takes and returns one part's arrays. A program takes and returns all parts, laid end to end along the dimension named above; an argument that names none is the same for every part. Nothing has to cross between parts.
Inputs may be any that keep to these rules, and one draw needn't show every extreme that they name: `key_chain`: never falling along the residues; each of the 24 chains holds at least one residue.
All inputs are finite; a program needn't handle non-finite values. No bound on the sum of `query_mask` or of `key_mask` on one device may be relied on, other than what follows from the above.
Results may differ from the reference program's by a relative error of at most 0.0082.
Values may be sent and summed in bfloat16 or wider, within the bound.
A program may use at most 64 MiB of HBM per device.

```python
import math
import jax
import jax.numpy as jnp
import numpy as np
from jax import lax

HEADS = 12
HEAD_DIM = 64
C = 128
RANK = 8
STEPS = 50
CHAINS = 24
SLABS = 2
D = 768
SLAB_ROWS = 16
RES = 1152


def scaled_entries(key, full_shape):
    return jnp.clip(jax.random.normal(key, full_shape, jnp.float32), -6.0, 6.0)


def draw_query_single(key, part):
    return scaled_entries(jax.random.fold_in(key, 11), (SLABS, SLAB_ROWS, D)).astype(jnp.bfloat16)


def draw_key_single(key, part):
    return scaled_entries(jax.random.fold_in(key, 12), (RES, D)).astype(jnp.bfloat16)


def draw_pair_block(key, part):
    base_key = jax.random.fold_in(key, 13)
    full_shape = (SLABS, SLAB_ROWS, RES, C)
    return jnp.clip(jax.random.normal(base_key, full_shape, jnp.float32), -6.0, 6.0)


def with_ends(array, own_key, least, top_value):
    extent = array.shape
    place = [jax.random.randint(jax.random.fold_in(own_key, axis), (), 0, extent[axis]) for axis in range(len(extent))]
    array = array.at[tuple(place)].set(least)
    longest = extent.index(max(extent))
    place[longest] = (place[longest] + 1) % extent[longest]
    return array.at[tuple(place)].set(top_value)


def steps_of(key, shape, cuts, low, largest):
    level = 1.0
    for axis_at, shards_of in cuts:
        steps = jax.random.uniform(jax.random.fold_in(jax.random.fold_in(key, 6), axis_at), (shards_of,), jnp.float32, low / len(cuts), largest / len(cuts))
        level = level * jnp.repeat(jnp.exp(steps), shape[axis_at] // shards_of).reshape((-1,) + (1,) * (len(shape) - 1 - axis_at))
    return level


def length_profile(number_of, total, bound, lean):
    loads = [(1 << 20) // math.isqrt(standing ** lean) + 1 for standing in range(2, number_of + 1)]
    rest, counts = total - bound - (number_of - 1), [1] * (number_of - 1)
    while rest > 0:
        candidates = [i for i in range(number_of - 1) if counts[i] < bound]
        pool, left = sum([loads[i] for i in candidates]), rest
        for i in candidates:
            more = min(bound - counts[i], max(1, left * loads[i] // pool), rest)
            counts[i] = counts[i] + more
            rest = rest - more
    return np.array([bound] + counts)


def ragged(stream_key, count, total, bound, slope):
    if count == 2:
        one = jax.random.randint(stream_key, (), max(1, total - bound), min(bound, total - 1) + 1)
        return jnp.stack([one, total - one])
    tallies = jnp.asarray(length_profile(count, total, bound, slope), jnp.int32)
    twos = (count - 1) // 2
    giver, receiver = tallies[1:1 + 2 * twos:2], tallies[2:2 + 2 * twos:2]
    slack = jnp.minimum(giver - 1, bound - receiver)
    shifted = jax.random.randint(jax.random.fold_in(stream_key, 1), (twos,), 0, 1 << 20) % (slack + 1)
    tallies = tallies.at[1:1 + 2 * twos:2].set(giver - shifted).at[2:2 + 2 * twos:2].set(receiver + shifted)
    return tallies[jax.random.permutation(jax.random.fold_in(stream_key, 2), count)]


def bell_draw(key, dims, scale, most, pieces=(), kind=jnp.bfloat16):
    drawn = scale * jax.random.normal(key, dims, jnp.float32)
    if pieces:
        drawn = drawn * steps_of(key, dims, pieces, -0.22, 0.18)
    return jnp.clip(drawn, -most, most).astype(kind)


def setup_inputs(seed: int = 0, part: int = 0) -> dict:
    streams_of = jax.random.split(jax.random.key(seed), 19)
    part_keys = jax.random.split(jax.random.fold_in(streams_of[18], part), 19)
    pair_block = draw_pair_block(jax.random.fold_in(jax.random.fold_in(streams_of[18], part), 71), part)
    query_single = draw_query_single(jax.random.fold_in(jax.random.fold_in(streams_of[18], part), 71), part)
    key_single = draw_key_single(jax.random.fold_in(jax.random.fold_in(streams_of[18], part), 71), part)
    query_chain = with_ends(jax.random.randint(part_keys[3], (SLABS, SLAB_ROWS), 0, CHAINS), jax.random.fold_in(part_keys[3], 1), 0, CHAINS - 1).astype(jnp.int32)
    key_chain = jnp.searchsorted(jnp.cumsum(ragged(part_keys[4], CHAINS, RES, RES // 8, 0)), jnp.arange(RES), side="right").astype(jnp.int32)
    query_mask = with_ends((jax.random.randint(part_keys[5], (SLABS, SLAB_ROWS), 0, 2) < 1).astype(jnp.int32), jax.random.fold_in(part_keys[5], 1), 0, 1)
    key_mask = with_ends((jax.random.randint(part_keys[6], (RES,), 0, 2) < 1).astype(jnp.int32), jax.random.fold_in(part_keys[6], 1), 0, 1)
    timestep = jax.random.randint(part_keys[7], (1,), 0, STEPS).astype(jnp.int32)
    time_table = bell_draw(streams_of[8], (STEPS, D), 1.0, 6.0)
    norm_gain = jnp.clip(1.0 + 0.18 * jax.random.normal(streams_of[9], (D,), jnp.float32), 0.1, 1.9)
    left_proj = bell_draw(streams_of[10], (D, RANK), D ** -0.5, 0.21875)
    right_proj = bell_draw(streams_of[11], (D, RANK), D ** -0.5, 0.21875)
    outer_proj = bell_draw(streams_of[12], (RANK * RANK, C), (RANK * RANK) ** -0.5, 0.75)
    bias_proj = bell_draw(streams_of[13], (C, HEADS), (C // 2) ** -0.5, 0.75, (), jnp.float32)
    chain_weight = jnp.clip(jax.random.uniform(streams_of[14], (HEADS,), jnp.float32, -2.0, 2.0), -2.0, 2.0)
    query_proj = bell_draw(streams_of[15], (D, 2 * D), D ** -0.5, 0.21875, ((1, 8),))
    kv_proj = bell_draw(streams_of[16], (D, 2 * D), D ** -0.5, 0.21875, ((1, 2),))
    out_proj = bell_draw(streams_of[17], (D, D), HEAD_DIM ** -0.5, 0.75)
    return dict(pair_block=pair_block, query_single=query_single, key_single=key_single, query_chain=query_chain, key_chain=key_chain, query_mask=query_mask, key_mask=key_mask, timestep=timestep, time_table=time_table, norm_gain=norm_gain, left_proj=left_proj, right_proj=right_proj, outer_proj=outer_proj, bias_proj=bias_proj, chain_weight=chain_weight, query_proj=query_proj, kv_proj=kv_proj, out_proj=out_proj)


EPSILON = 1e-05
HIGHEST = lax.Precision.HIGHEST

def normalize(features, norm_gain):
    average = lax.optimization_barrier(jnp.mean(features, axis=-1, keepdims=True))
    centred = features - average
    spread = lax.optimization_barrier(jnp.mean(centred * centred, axis=-1, keepdims=True))
    return (centred * lax.rsqrt(spread + EPSILON) * norm_gain).astype(jnp.bfloat16)

def wide_dot(left, right):
    return jnp.dot(left.astype(jnp.float32), right.astype(jnp.float32), precision=HIGHEST, preferred_element_type=jnp.float32)

def flat_dot(left, right):
    flat_left = left.reshape(-1, left.shape[-1])
    product = wide_dot(flat_left, right)
    return product.reshape(left.shape[:-1] + (right.shape[-1],))

def reference(pair_block, query_single, key_single, query_chain, key_chain, query_mask, key_mask, timestep, time_table, norm_gain, left_proj, right_proj, outer_proj, bias_proj, chain_weight, query_proj, kv_proj, out_proj):
    picked = jnp.arange(STEPS, dtype=jnp.int32) == timestep[0]
    time_row = lax.optimization_barrier(jnp.sum(jnp.where(picked[:, None], time_table.astype(jnp.float32), jnp.float32(0.0)), axis=0))
    query_norm = normalize(query_single.astype(jnp.float32) + query_mask[:, :, None].astype(jnp.float32) * time_row, norm_gain)
    key_norm = normalize(key_single.astype(jnp.float32) + key_mask[:, None].astype(jnp.float32) * time_row, norm_gain)
    query_gate = lax.optimization_barrier(flat_dot(query_norm, query_proj).astype(jnp.bfloat16))
    keys_values = lax.optimization_barrier(wide_dot(key_norm, kv_proj).astype(jnp.bfloat16))
    left_factor = flat_dot(query_norm, left_proj)
    right_factor = wide_dot(key_norm, right_proj)
    mixer = jnp.einsum('sra,abc->srbc', left_factor, outer_proj.astype(jnp.float32).reshape(RANK, RANK, C), precision=HIGHEST)
    new_pair = pair_block + jnp.einsum('jb,srbc->srjc', right_factor, mixer, precision=HIGHEST)
    differ = (query_chain[:, :, None] != key_chain[None, None, :]).astype(jnp.float32)
    logit_bias = jnp.einsum('srjc,ch->srhj', new_pair, bias_proj, precision=HIGHEST) + chain_weight[None, None, :, None] * differ[:, :, None, :]
    query_heads = query_gate[:, :, :D].astype(jnp.float32).reshape(SLABS, SLAB_ROWS, HEADS, HEAD_DIM)
    key_heads = keys_values[:, :D].astype(jnp.float32).reshape(RES, HEADS, HEAD_DIM)
    value_heads = keys_values[:, D:].astype(jnp.float32).reshape(RES, HEADS, HEAD_DIM)
    scores = jnp.einsum('srhd,jhd->srhj', query_heads, key_heads, precision=HIGHEST) * (1.0 / math.sqrt(HEAD_DIM)) + logit_bias
    maxima = lax.optimization_barrier(jnp.max(scores, axis=-1, keepdims=True))
    exponent = jnp.exp(scores - maxima)
    totals = lax.optimization_barrier(jnp.sum(exponent, axis=-1))
    weights = lax.optimization_barrier(exponent.astype(jnp.bfloat16)).astype(jnp.float32)
    summed = jnp.einsum('srhj,jhd->srhd', weights, value_heads, precision=HIGHEST)
    gate_factor = jax.nn.sigmoid(query_gate[:, :, D:].astype(jnp.float32))
    attended = ((summed / totals[..., None]).reshape(SLABS, SLAB_ROWS, D) * gate_factor).astype(jnp.bfloat16)
    single_update = flat_dot(attended, out_proj).astype(jnp.bfloat16)
    return (new_pair, single_update)
```

```python
import functools
import math

import jax
import jax.numpy as jnp
from jax import lax
from jax.experimental import pallas as pl
from jax.experimental.pallas import tpu as pltpu
from jax.sharding import PartitionSpec as P

EPSILON = 1e-05
HIGHEST = lax.Precision.HIGHEST


def combined_all(part, axis, combine):
    gathered = jax.tree.map(lambda a: lax.all_gather(a, axis), part)

    def take(source):
        return jax.tree.map(lambda a: lax.dynamic_index_in_dim(a, source, 0, False), gathered)

    return lax.fori_loop(
        1, lax.axis_size(axis), lambda source, state: combine(state, take(source)), take(0)
    )


def normalize(features, norm_gain):
    average = jnp.mean(features, axis=-1, keepdims=True)
    centred = features - average
    spread = jnp.mean(centred * centred, axis=-1, keepdims=True)
    return (centred * lax.rsqrt(spread + EPSILON) * norm_gain).astype(jnp.bfloat16)


def flat_dot(left, right):
    flat_left = left.reshape(-1, left.shape[-1])
    product = jnp.dot(flat_left, right, preferred_element_type=jnp.float32)
    return product.reshape(left.shape[:-1] + (right.shape[-1],))


def combine_parts(former, latter):
    peak_former, total_former, summed_former = former
    peak_latter, total_latter, summed_latter = latter
    peak_joint = jnp.maximum(peak_former, peak_latter)
    scale_former = jnp.exp(peak_former - peak_joint)
    scale_latter = jnp.exp(peak_latter - peak_joint)
    head_width = summed_former.shape[-1] // peak_joint.shape[-1]
    total_joint = total_former * scale_former + total_latter * scale_latter
    summed_joint = summed_former * jnp.repeat(
        scale_former, head_width, axis=-1
    ) + summed_latter * jnp.repeat(scale_latter, head_width, axis=-1)
    return (peak_joint, total_joint, summed_joint)


def local_parts(query_heads, key_heads, value_heads, logit_bias):
    scores = (
        jnp.einsum("srhd,jhd->srhj", query_heads, key_heads, preferred_element_type=jnp.float32)
        * (1.0 / math.sqrt(query_heads.shape[-1]))
        + logit_bias
    )
    maxima = jnp.max(scores, axis=-1)
    exponent = jnp.exp(scores - maxima[..., None])
    totals = jnp.sum(exponent, axis=-1)
    summed = jnp.einsum(
        "srhj,jhd->srhd",
        exponent.astype(jnp.bfloat16),
        value_heads,
        preferred_element_type=jnp.float32,
    )
    return (maxima, totals, summed.reshape(summed.shape[0], summed.shape[1], -1))


def finish(partials, gate_factor, out_proj, heads):
    maxima, totals, summed = combined_all(partials, "col", combine_parts)
    head_width = summed.shape[-1] // heads
    attended = (summed / jnp.repeat(totals, head_width, axis=-1) * gate_factor).astype(jnp.bfloat16)
    return flat_dot(attended, out_proj).astype(jnp.bfloat16)


def on_device(
    pair_block,
    query_single,
    key_single,
    query_chain,
    key_chain,
    query_mask,
    key_mask,
    timestep,
    time_table,
    norm_gain,
    left_proj,
    right_proj,
    outer_proj,
    bias_proj,
    chain_weight,
    query_proj,
    kv_proj,
    out_proj,
):
    step_count = time_table.shape[0]
    picked = jnp.arange(step_count, dtype=jnp.int32) == timestep[0]
    time_row = jnp.sum(
        jnp.where(picked[:, None], time_table.astype(jnp.float32), jnp.float32(0.0)), axis=0
    )
    query_norm = normalize(
        query_single.astype(jnp.float32) + query_mask[:, :, None].astype(jnp.float32) * time_row,
        norm_gain,
    )
    key_norm = normalize(
        key_single.astype(jnp.float32) + key_mask[:, None].astype(jnp.float32) * time_row, norm_gain
    )
    query_part = flat_dot(query_norm, query_proj).astype(jnp.bfloat16)
    query_gate = lax.all_gather(query_part, "col", axis=2, tiled=True)
    half_projected = jnp.dot(key_norm, kv_proj, preferred_element_type=jnp.float32).astype(
        jnp.bfloat16
    )
    keys_values = lax.all_gather(half_projected, "row", axis=1, tiled=True)
    rank = left_proj.shape[1]
    channels = outer_proj.shape[1]
    left_factor = flat_dot(query_norm, left_proj)
    right_factor = jnp.dot(key_norm, right_proj, preferred_element_type=jnp.float32)
    mixer = jnp.einsum(
        "sra,abc->srbc",
        left_factor,
        outer_proj.astype(jnp.float32).reshape(rank, rank, channels),
        precision=HIGHEST,
    )
    new_pair = pair_block + jnp.einsum("jb,srbc->srjc", right_factor, mixer, precision=HIGHEST)
    differ = (query_chain[:, :, None] != key_chain[None, None, :]).astype(jnp.float32)
    logit_bias = (
        jnp.einsum("srjc,ch->srhj", new_pair, bias_proj, precision=HIGHEST)
        + chain_weight[None, None, :, None] * differ[:, :, None, :]
    )
    heads = chain_weight.shape[0]
    model_width = query_norm.shape[-1]
    head_size = model_width // heads
    slab_count = query_gate.shape[0]
    slab_rows = query_gate.shape[1]
    key_count = keys_values.shape[0]
    query_heads = query_gate[:, :, :model_width].reshape(slab_count, slab_rows, heads, head_size)
    gate_factor = jax.nn.sigmoid(query_gate[:, :, model_width:].astype(jnp.float32))
    key_heads = keys_values[:, :model_width].reshape(key_count, heads, head_size)
    value_heads = keys_values[:, model_width:].reshape(key_count, heads, head_size)
    single_update = finish(
        local_parts(query_heads, key_heads, value_heads, logit_bias), gate_factor, out_proj, heads
    )
    return (new_pair, single_update)


def iota(shape, axis):
    return lax.broadcasted_iota(jnp.int32, shape, axis)


def dot_nt(left, right, precision=None):
    return lax.dot_general(
        left, right, (((1,), (1,)), ((), ())), precision=precision,
        preferred_element_type=jnp.float32,
    )


def dot_nn(left, right, precision=None):
    return jnp.dot(left, right, precision=precision, preferred_element_type=jnp.float32)


def rounded(value):
    return value.astype(jnp.bfloat16).astype(jnp.float32)


def column_of(row, count):
    spot = iota((count, row.shape[1]), 0) == iota((count, row.shape[1]), 1)
    return jnp.sum(jnp.where(spot, row, jnp.zeros_like(row)), axis=1, keepdims=True)


def fused_kernel(
    query_chain, timestep, query_single, key_single, key_chain, query_mask, key_mask,
    time_table, norm_gain, left_proj, right_proj, outer_proj, bias_proj, chain_weight,
    pair_hbm, query_proj_hbm, kv_proj_hbm, out_proj_hbm,
    new_pair_hbm, single_update,
    pair, fresh, query_proj, kv_proj, out_proj, parts_q, keys_values, bias, mixers,
    packed, partial, gates, final,
    load_sem, store_sem, q_send, q_recv, kv_send, kv_recv, p_send, p_recv, f_send, f_recv,
):
    cols = lax.axis_size("col")
    me = lax.axis_index("col")
    side = lax.axis_index("row")
    peers = [lax.rem(me + offset, cols) for offset in range(1, cols)]

    barrier = pltpu.get_barrier_semaphore()
    for peer in peers:
        pl.semaphore_signal(
            barrier, inc=1, device_id={"col": peer}, device_id_type=pl.DeviceIdType.MESH
        )
    pl.semaphore_signal(
        barrier, inc=1, device_id={"row": 1 - side}, device_id_type=pl.DeviceIdType.MESH
    )

    loads = [
        pltpu.make_async_copy(source, target, load_sem.at[place])
        for place, (source, target) in enumerate(
            [
                (query_proj_hbm, query_proj),
                (kv_proj_hbm, kv_proj),
                (pair_hbm, pair),
                (out_proj_hbm, out_proj),
            ]
        )
    ]
    for load in loads:
        load.start()

    slabs, slab_rows, width = query_single.shape
    rows = slabs * slab_rows
    keys = key_single.shape[0]
    steps = time_table.shape[0]
    rank = left_proj.shape[1]
    channels = outer_proj.shape[1]
    heads = chain_weight.shape[1]
    head_width = width // heads
    slots = bias.shape[2]
    own_rows = rows // cols

    def normal(features):
        average = jnp.mean(features, axis=-1, keepdims=True)
        centred = features - average
        spread = jnp.mean(centred * centred, axis=-1, keepdims=True)
        return (centred * lax.rsqrt(spread + EPSILON) * norm_gain[...]).astype(jnp.bfloat16)

    picked = iota((steps, width), 0) == timestep[0]
    time_row = jnp.sum(
        jnp.where(picked, time_table[...].astype(jnp.float32), 0.0), axis=0, keepdims=True
    )

    query_flags = jnp.concatenate(
        [
            column_of(query_mask[slab : slab + 1, :].astype(jnp.float32), slab_rows)
            for slab in range(slabs)
        ],
        axis=0,
    )
    query_norm = normal(
        query_single[...].astype(jnp.float32).reshape(rows, width) + query_flags * time_row
    )
    loads[0].wait()
    parts_q[me] = dot_nn(query_norm, query_proj[...]).astype(jnp.bfloat16)

    pl.semaphore_wait(barrier, cols)
    q_copies = [
        pltpu.make_async_remote_copy(
            src_ref=parts_q.at[me], dst_ref=parts_q.at[me],
            send_sem=q_send.at[place], recv_sem=q_recv.at[place],
            device_id={"col": peer}, device_id_type=pl.DeviceIdType.MESH,
        )
        for place, peer in enumerate(peers)
    ]
    for copy in q_copies:
        copy.start()

    key_flags = column_of(key_mask[...].astype(jnp.float32), keys)
    key_norm = normal(key_single[...].astype(jnp.float32) + key_flags * time_row)
    loads[1].wait()
    keys_values[side] = dot_nn(key_norm, kv_proj[...]).astype(jnp.bfloat16)
    kv_copy = pltpu.make_async_remote_copy(
        src_ref=keys_values.at[side], dst_ref=keys_values.at[side],
        send_sem=kv_send, recv_sem=kv_recv,
        device_id={"row": 1 - side}, device_id_type=pl.DeviceIdType.MESH,
    )
    kv_copy.start()

    left_factor = dot_nn(query_norm, left_proj[...])
    right_factor = dot_nn(key_norm, right_proj[...])
    square = rank * rank
    spread_left = (iota((rank, square), 1) // rank == iota((rank, square), 0)).astype(jnp.float32)
    left_wide = dot_nn(left_factor, spread_left, HIGHEST)
    on_rank = iota((rows, rank, square), 2) % rank == iota((rows, rank, square), 1)
    left_blocks = jnp.where(on_rank, left_wide[:, None, :], 0.0).reshape(rows * rank, square)
    mixer = dot_nn(left_blocks, outer_proj[...].astype(jnp.float32), HIGHEST)
    mixer = mixer.reshape(rows, rank, channels)

    terms = 6
    tile_right = (iota((rank, terms * rank), 1) % rank == iota((rank, terms * rank), 0)).astype(
        jnp.float32
    )
    right_wide = dot_nn(right_factor, tile_right, HIGHEST)
    right_1 = rounded(right_wide)
    right_2 = rounded(right_wide - right_1)
    right_3 = right_wide - right_1 - right_2
    group = iota(right_wide.shape, 1) // rank
    right_terms = jnp.where(
        group < 3, right_1, jnp.where(group < 5, right_2, right_3)
    ).astype(jnp.bfloat16)
    mixer_1 = rounded(mixer)
    mixer_2 = rounded(mixer - mixer_1)
    mixer_3 = mixer - mixer_1 - mixer_2
    mixers[...] = jnp.concatenate(
        [mixer_1, mixer_2, mixer_3, mixer_1, mixer_2, mixer_1], axis=1
    ).astype(jnp.bfloat16)

    head_spot = (iota((slots, heads), 0) == iota((slots, heads), 1)).astype(jnp.float32)
    bias_rows = dot_nt(head_spot, bias_proj[...], HIGHEST)
    bias_1 = rounded(bias_rows)
    bias_2 = bias_rows - bias_1
    bias_terms = jnp.concatenate(
        [
            jnp.concatenate([bias_1, bias_1], axis=1),
            jnp.concatenate([bias_2, bias_2], axis=1),
        ],
        axis=0,
    ).astype(jnp.bfloat16)
    chain_column = column_of(chain_weight[...], slots)
    chains = key_chain[...]

    loads[2].wait()

    def update_row(row, carry):
        slab = row // slab_rows
        place = row - slab * slab_rows
        updated = pair[slab, place] + dot_nn(right_terms, mixers[row])
        fresh[slab, place] = updated
        upper = rounded(updated)
        both = jnp.concatenate([upper, updated - upper], axis=1).astype(jnp.bfloat16)
        logits = dot_nt(bias_terms, both)
        differ = (chains != query_chain[slab, place]).astype(jnp.float32)
        bias[slab, place] = logits[:slots] + logits[slots:] + chain_column * differ
        return carry

    lax.fori_loop(0, rows, update_row, 0, unroll=UNROLL)
    store = pltpu.make_async_copy(fresh, new_pair_hbm, store_sem)
    store.start()

    for copy in q_copies:
        copy.wait()
    half = cols // 2
    query = jnp.concatenate(
        [parts_q[place].astype(jnp.float32) for place in range(half)], axis=1
    )
    gate = jax.nn.sigmoid(
        jnp.concatenate(
            [parts_q[place].astype(jnp.float32) for place in range(half, cols)], axis=1
        )
    )
    for place in range(cols):
        gates[place] = gate[place * own_rows : (place + 1) * own_rows]
    on_head = iota((rows, slots, width), 2) // head_width == iota((rows, slots, width), 1)
    query_blocks = (
        jnp.where(on_head, query[:, None, :], 0.0)
        .reshape(rows * slots, width)
        .astype(jnp.bfloat16)
    )
    kv_copy.wait()
    scores = dot_nt(query_blocks, keys_values[0]) * (1.0 / math.sqrt(head_width)) + bias[
        ...
    ].reshape(rows * slots, keys)
    maxima = jnp.max(scores, axis=1, keepdims=True)
    exponent = jnp.exp(scores - maxima)
    totals = jnp.sum(exponent, axis=1, keepdims=True)
    summed = dot_nn(exponent.astype(jnp.bfloat16), keys_values[1]).reshape(rows, slots, width)
    summed = jnp.sum(jnp.where(on_head, summed, 0.0), axis=1)
    on_lane = iota((rows, slots, LANES), 2) == iota((rows, slots, LANES), 1)

    def by_lane(column):
        return jnp.sum(jnp.where(on_lane, column.reshape(rows, slots, 1), 0.0), axis=1)

    bundle = jnp.concatenate([summed, by_lane(maxima), by_lane(totals)], axis=1)
    for place in range(cols):
        packed[place] = bundle[place * own_rows : (place + 1) * own_rows]
    p_copies = [
        pltpu.make_async_remote_copy(
            src_ref=packed.at[peer], dst_ref=partial.at[me],
            send_sem=p_send.at[place], recv_sem=p_recv.at[place],
            device_id={"col": peer}, device_id_type=pl.DeviceIdType.MESH,
        )
        for place, peer in enumerate(peers)
    ]
    for copy in p_copies:
        copy.start()
    partial[me] = packed[me]
    gate_own = gates[me]
    spread_heads = (
        (iota((LANES, width), 1) // head_width == iota((LANES, width), 0))
        .astype(jnp.float32)
    )
    loads[3].wait()
    for copy in p_copies:
        copy.wait()

    maxima = [partial[place, :, width : width + LANES] for place in range(cols)]
    totals = [partial[place, :, width + LANES :] for place in range(cols)]
    peak = functools.reduce(jnp.maximum, maxima)
    scales = [jnp.exp(part - peak) for part in maxima]
    total = functools.reduce(jnp.add, [a * b for a, b in zip(totals, scales)])
    total = jnp.where(iota(total.shape, 1) < heads, total, 1.0)
    shares = dot_nn(
        jnp.concatenate([scale / total for scale in scales], axis=0), spread_heads, HIGHEST
    )
    joint = functools.reduce(
        jnp.add,
        [
            shares[place * own_rows : (place + 1) * own_rows] * partial[place, :, :width]
            for place in range(cols)
        ],
    )
    attended = joint * gate_own
    attended = jnp.concatenate(
        [attended, jnp.zeros((rows - own_rows, width), jnp.float32)], axis=0
    ).astype(jnp.bfloat16)

    final[me] = rounded(dot_nn(attended, out_proj[...])[:own_rows])
    f_copies = [
        pltpu.make_async_remote_copy(
            src_ref=final.at[me], dst_ref=final.at[me],
            send_sem=f_send.at[place], recv_sem=f_recv.at[place],
            device_id={"col": peer}, device_id_type=pl.DeviceIdType.MESH,
        )
        for place, peer in enumerate(peers)
    ]
    for copy in f_copies:
        copy.start()
    store.wait()
    for copy in f_copies:
        copy.wait()
    single_update[...] = (
        jnp.concatenate([final[place] for place in range(cols)], axis=0)
        .reshape(slabs, slab_rows, width)
        .astype(jnp.bfloat16)
    )


LANES = 128
UNROLL = 4


def fused(
    pair_block, query_single, key_single, query_chain, key_chain, query_mask, key_mask,
    timestep, time_table, norm_gain, left_proj, right_proj, outer_proj, bias_proj,
    chain_weight, query_proj, kv_proj, out_proj,
):
    cols = lax.axis_size("col")
    slabs, slab_rows, width = query_single.shape
    rows = slabs * slab_rows
    keys = key_single.shape[0]
    heads = chain_weight.shape[0]
    slots = -(-heads // 16) * 16
    rank = left_proj.shape[1]
    own_rows = rows // cols
    vmem = pl.BlockSpec(memory_space=pltpu.VMEM)
    smem = pl.BlockSpec(memory_space=pltpu.SMEM)
    anywhere = pl.BlockSpec(memory_space=pl.ANY)
    dma = pltpu.SemaphoreType.DMA
    return pl.pallas_call(
        fused_kernel,
        out_shape=(
            jax.ShapeDtypeStruct(pair_block.shape, jnp.float32),
            jax.ShapeDtypeStruct(query_single.shape, jnp.bfloat16),
        ),
        in_specs=[smem, smem] + [vmem] * 12 + [anywhere] * 4,
        out_specs=(anywhere, vmem),
        scratch_shapes=[
            pltpu.VMEM(pair_block.shape, jnp.float32),
            pltpu.VMEM(pair_block.shape, jnp.float32),
            pltpu.VMEM(query_proj.shape, jnp.bfloat16),
            pltpu.VMEM(kv_proj.shape, jnp.bfloat16),
            pltpu.VMEM(out_proj.shape, jnp.bfloat16),
            pltpu.VMEM((cols, rows, query_proj.shape[1]), jnp.bfloat16),
            pltpu.VMEM((2, keys, width), jnp.bfloat16),
            pltpu.VMEM((slabs, slab_rows, slots, keys), jnp.float32),
            pltpu.VMEM((rows, 6 * rank, outer_proj.shape[1]), jnp.bfloat16),
            pltpu.VMEM((cols, own_rows, width + 2 * LANES), jnp.float32),
            pltpu.VMEM((cols, own_rows, width + 2 * LANES), jnp.float32),
            pltpu.VMEM((cols, own_rows, width), jnp.float32),
            pltpu.VMEM((cols, own_rows, width), jnp.float32),
            dma((4,)),
            dma,
            dma((cols - 1,)),
            dma((cols - 1,)),
            dma,
            dma,
            dma((cols - 1,)),
            dma((cols - 1,)),
            dma((cols - 1,)),
            dma((cols - 1,)),
        ],
        compiler_params=pltpu.CompilerParams(
            collective_id=0, has_side_effects=True, vmem_limit_bytes=48 * 1024 * 1024
        ),
    )(
        query_chain, timestep, query_single, key_single, key_chain.reshape(1, -1), query_mask,
        key_mask.reshape(1, -1), time_table, norm_gain.reshape(1, -1), left_proj, right_proj,
        outer_proj, bias_proj, chain_weight.reshape(1, -1), pair_block, query_proj, kv_proj,
        out_proj,
    )


def serve(*arrays):
    query_single, chain_weight, kv_proj = arrays[1], arrays[14], arrays[16]
    rows = query_single.shape[0] * query_single.shape[1]
    cols = lax.axis_size("col")
    fits = (
        rows % cols == 0
        and cols % 2 == 0
        and lax.axis_size("row") == 2
        and kv_proj.shape[1] == query_single.shape[2]
        and chain_weight.shape[0] <= LANES
    )
    return fused(*arrays) if fits else on_device(*arrays)


def solution(mesh):
    return jax.shard_map(
        serve,
        mesh=mesh,
        in_specs=(
            P("grp", "row", "col", None),
            P("grp", "row", None),
            P(("grp", "col"), None),
            P("grp", "row"),
            P(("grp", "col")),
            P("grp", "row"),
            P(("grp", "col")),
            P("grp"),
            P(),
            P(),
            P(),
            P(),
            P(),
            P(),
            P(),
            P(None, "col"),
            P(None, "row"),
            P(),
        ),
        out_specs=(P("grp", "row", "col", None), P("grp", "row", None)),
        check_vma=False,
    )
```

```python
import functools
import math

import jax
import jax.numpy as jnp
from jax import lax
from jax.experimental import pallas as pl
from jax.experimental.pallas import tpu as pltpu
from jax.sharding import PartitionSpec as P

EPSILON = 1e-05
HIGHEST = lax.Precision.HIGHEST


def combined_all(part, axis, combine):
    gathered = jax.tree.map(lambda a: lax.all_gather(a, axis), part)

    def take(source):
        return jax.tree.map(lambda a: lax.dynamic_index_in_dim(a, source, 0, False), gathered)

    return lax.fori_loop(
        1, lax.axis_size(axis), lambda source, state: combine(state, take(source)), take(0)
    )


def normalize(features, norm_gain):
    average = jnp.mean(features, axis=-1, keepdims=True)
    centred = features - average
    spread = jnp.mean(centred * centred, axis=-1, keepdims=True)
    return (centred * lax.rsqrt(spread + EPSILON) * norm_gain).astype(jnp.bfloat16)


def flat_dot(left, right):
    flat_left = left.reshape(-1, left.shape[-1])
    product = jnp.dot(flat_left, right, preferred_element_type=jnp.float32)
    return product.reshape(left.shape[:-1] + (right.shape[-1],))


def combine_parts(former, latter):
    peak_former, total_former, summed_former = former
    peak_latter, total_latter, summed_latter = latter
    peak_joint = jnp.maximum(peak_former, peak_latter)
    scale_former = jnp.exp(peak_former - peak_joint)
    scale_latter = jnp.exp(peak_latter - peak_joint)
    head_width = summed_former.shape[-1] // peak_joint.shape[-1]
    total_joint = total_former * scale_former + total_latter * scale_latter
    summed_joint = summed_former * jnp.repeat(
        scale_former, head_width, axis=-1
    ) + summed_latter * jnp.repeat(scale_latter, head_width, axis=-1)
    return (peak_joint, total_joint, summed_joint)


def local_parts(query_heads, key_heads, value_heads, logit_bias):
    scores = (
        jnp.einsum("srhd,jhd->srhj", query_heads, key_heads, preferred_element_type=jnp.float32)
        * (1.0 / math.sqrt(query_heads.shape[-1]))
        + logit_bias
    )
    maxima = jnp.max(scores, axis=-1)
    exponent = jnp.exp(scores - maxima[..., None])
    totals = jnp.sum(exponent, axis=-1)
    summed = jnp.einsum(
        "srhj,jhd->srhd",
        exponent.astype(jnp.bfloat16),
        value_heads,
        preferred_element_type=jnp.float32,
    )
    return (maxima, totals, summed.reshape(summed.shape[0], summed.shape[1], -1))


def finish(partials, gate_factor, out_proj, heads):
    maxima, totals, summed = combined_all(partials, "col", combine_parts)
    head_width = summed.shape[-1] // heads
    attended = (summed / jnp.repeat(totals, head_width, axis=-1) * gate_factor).astype(jnp.bfloat16)
    return flat_dot(attended, out_proj).astype(jnp.bfloat16)


def on_device(
    pair_block,
    query_single,
    key_single,
    query_chain,
    key_chain,
    query_mask,
    key_mask,
    timestep,
    time_table,
    norm_gain,
    left_proj,
    right_proj,
    outer_proj,
    bias_proj,
    chain_weight,
    query_proj,
    kv_proj,
    out_proj,
):
    step_count = time_table.shape[0]
    picked = jnp.arange(step_count, dtype=jnp.int32) == timestep[0]
    time_row = jnp.sum(
        jnp.where(picked[:, None], time_table.astype(jnp.float32), jnp.float32(0.0)), axis=0
    )
    query_norm = normalize(
        query_single.astype(jnp.float32) + query_mask[:, :, None].astype(jnp.float32) * time_row,
        norm_gain,
    )
    key_norm = normalize(
        key_single.astype(jnp.float32) + key_mask[:, None].astype(jnp.float32) * time_row, norm_gain
    )
    query_part = flat_dot(query_norm, query_proj).astype(jnp.bfloat16)
    query_gate = lax.all_gather(query_part, "col", axis=2, tiled=True)
    half_projected = jnp.dot(key_norm, kv_proj, preferred_element_type=jnp.float32).astype(
        jnp.bfloat16
    )
    keys_values = lax.all_gather(half_projected, "row", axis=1, tiled=True)
    rank = left_proj.shape[1]
    channels = outer_proj.shape[1]
    left_factor = flat_dot(query_norm, left_proj)
    right_factor = jnp.dot(key_norm, right_proj, preferred_element_type=jnp.float32)
    mixer = jnp.einsum(
        "sra,abc->srbc",
        left_factor,
        outer_proj.astype(jnp.float32).reshape(rank, rank, channels),
        precision=HIGHEST,
    )
    new_pair = pair_block + jnp.einsum("jb,srbc->srjc", right_factor, mixer, precision=HIGHEST)
    differ = (query_chain[:, :, None] != key_chain[None, None, :]).astype(jnp.float32)
    logit_bias = (
        jnp.einsum("srjc,ch->srhj", new_pair, bias_proj, precision=HIGHEST)
        + chain_weight[None, None, :, None] * differ[:, :, None, :]
    )
    heads = chain_weight.shape[0]
    model_width = query_norm.shape[-1]
    head_size = model_width // heads
    slab_count = query_gate.shape[0]
    slab_rows = query_gate.shape[1]
    key_count = keys_values.shape[0]
    query_heads = query_gate[:, :, :model_width].reshape(slab_count, slab_rows, heads, head_size)
    gate_factor = jax.nn.sigmoid(query_gate[:, :, model_width:].astype(jnp.float32))
    key_heads = keys_values[:, :model_width].reshape(key_count, heads, head_size)
    value_heads = keys_values[:, model_width:].reshape(key_count, heads, head_size)
    single_update = finish(
        local_parts(query_heads, key_heads, value_heads, logit_bias), gate_factor, out_proj, heads
    )
    return (new_pair, single_update)


def iota(shape, axis):
    return lax.broadcasted_iota(jnp.int32, shape, axis)


def dot_nt(left, right, precision=None):
    return lax.dot_general(
        left, right, (((1,), (1,)), ((), ())), precision=precision,
        preferred_element_type=jnp.float32,
    )


def dot_nn(left, right, precision=None):
    return jnp.dot(left, right, precision=precision, preferred_element_type=jnp.float32)


def rounded(value):
    return value.astype(jnp.bfloat16).astype(jnp.float32)


def column_of(row, count):
    spot = iota((count, row.shape[1]), 0) == iota((count, row.shape[1]), 1)
    return jnp.sum(jnp.where(spot, row, jnp.zeros_like(row)), axis=1, keepdims=True)


def fused_kernel(
    query_chain, timestep, *operands_results_scratch
):
    sources = operands_results_scratch[:OPERANDS]
    new_pair_hbm, single_update = operands_results_scratch[OPERANDS : OPERANDS + 2]
    targets = operands_results_scratch[OPERANDS + 2 : 2 * OPERANDS + 2]
    (
        time_table, query_single, query_mask, norm_gain, query_proj, key_single, key_mask,
        kv_proj, left_proj, right_proj, outer_proj, bias_proj, chain_weight, key_chain, pair,
        out_proj,
    ) = targets
    (
        fresh, parts_q, keys_values, bias, packed, partial, gates, final,
        load_sem, store_sem, q_send, q_recv, kv_send, kv_recv, p_send, p_recv, f_send, f_recv,
    ) = operands_results_scratch[2 * OPERANDS + 2 :]
    cols = lax.axis_size("col")
    me = lax.axis_index("col")
    side = lax.axis_index("row")
    peers = [lax.rem(me + offset, cols) for offset in range(1, cols)]

    loads = [
        pltpu.make_async_copy(source, target, load_sem.at[place])
        for place, (source, target) in enumerate(zip(sources, targets))
    ]
    for load in loads:
        load.start()

    barrier = pltpu.get_barrier_semaphore()
    for peer in peers:
        pl.semaphore_signal(
            barrier, inc=1, device_id={"col": peer}, device_id_type=pl.DeviceIdType.MESH
        )
    pl.semaphore_signal(
        barrier, inc=1, device_id={"row": 1 - side}, device_id_type=pl.DeviceIdType.MESH
    )

    slabs, slab_rows, width = query_single.shape
    rows = slabs * slab_rows
    keys = key_single.shape[0]
    steps = time_table.shape[0]
    rank = left_proj.shape[0]
    channels = outer_proj.shape[1]
    heads = chain_weight.shape[1]
    head_width = width // heads
    slots = bias.shape[2]
    own_rows = rows // cols

    for load in loads[:4]:
        load.wait()
    gain = jnp.concatenate(
        [norm_gain[place : place + 1] for place in range(norm_gain.shape[0])], axis=1
    )

    def normal(features):
        average = jnp.mean(features, axis=-1, keepdims=True)
        centred = features - average
        spread = jnp.mean(centred * centred, axis=-1, keepdims=True)
        return (centred * lax.rsqrt(spread + EPSILON) * gain).astype(jnp.bfloat16)

    picked = iota((steps, width), 0) == timestep[0]
    time_row = jnp.sum(
        jnp.where(picked, time_table[...].astype(jnp.float32), 0.0), axis=0, keepdims=True
    )

    query_flags = jnp.concatenate(
        [
            column_of(query_mask[slab : slab + 1, :].astype(jnp.float32), slab_rows)
            for slab in range(slabs)
        ],
        axis=0,
    )
    query_norm = normal(
        query_single[...].astype(jnp.float32).reshape(rows, width) + query_flags * time_row
    )
    loads[4].wait()
    parts_q[me] = dot_nt(query_norm, query_proj[...]).astype(jnp.bfloat16)

    pl.semaphore_wait(barrier, cols)
    q_copies = [
        pltpu.make_async_remote_copy(
            src_ref=parts_q.at[me], dst_ref=parts_q.at[me],
            send_sem=q_send.at[place], recv_sem=q_recv.at[place],
            device_id={"col": peer}, device_id_type=pl.DeviceIdType.MESH,
        )
        for place, peer in enumerate(peers)
    ]
    for copy in q_copies:
        copy.start()

    loads[5].wait()
    loads[6].wait()
    key_flags = column_of(key_mask[...].astype(jnp.float32), keys)
    key_norm = normal(key_single[...].astype(jnp.float32) + key_flags * time_row)
    loads[7].wait()
    keys_values[side] = dot_nn(key_norm, kv_proj[...]).astype(jnp.bfloat16)
    kv_copy = pltpu.make_async_remote_copy(
        src_ref=keys_values.at[side], dst_ref=keys_values.at[side],
        send_sem=kv_send, recv_sem=kv_recv,
        device_id={"row": 1 - side}, device_id_type=pl.DeviceIdType.MESH,
    )
    kv_copy.start()

    for load in loads[8:14]:
        load.wait()
    left_factor = dot_nt(query_norm, left_proj[...])
    right_factor = dot_nt(key_norm, right_proj[...])
    square = rank * rank
    spread_left = (iota((rank, square), 1) // rank == iota((rank, square), 0)).astype(jnp.float32)
    left_wide = dot_nn(left_factor, spread_left, HIGHEST)
    on_rank = iota((rows, rank, square), 2) % rank == iota((rows, rank, square), 1)
    left_blocks = jnp.where(on_rank, left_wide[:, None, :], 0.0).reshape(rows * rank, square)
    mixer = dot_nn(left_blocks, outer_proj[...].astype(jnp.float32), HIGHEST)
    mixer = jnp.concatenate(
        [mixer[row * rank : (row + 1) * rank] for row in range(rows)], axis=1
    )

    terms = 6
    tile_right = (iota((rank, terms * rank), 1) % rank == iota((rank, terms * rank), 0)).astype(
        jnp.float32
    )
    right_wide = dot_nn(right_factor, tile_right, HIGHEST)
    right_1 = rounded(right_wide)
    right_2 = rounded(right_wide - right_1)
    right_3 = right_wide - right_1 - right_2
    group = iota(right_wide.shape, 1) // rank
    right_terms = jnp.where(
        group < 3, right_1, jnp.where(group < 5, right_2, right_3)
    ).astype(jnp.bfloat16)
    mixer_1 = rounded(mixer)
    mixer_2 = rounded(mixer - mixer_1)
    mixer_3 = mixer - mixer_1 - mixer_2
    mixer_terms = jnp.concatenate(
        [mixer_1, mixer_2, mixer_3, mixer_1, mixer_2, mixer_1], axis=0
    ).astype(jnp.bfloat16)

    head_spot = (iota((slots, heads), 0) == iota((slots, heads), 1)).astype(jnp.float32)
    bias_rows = dot_nn(head_spot, bias_proj[...], HIGHEST)
    bias_1 = rounded(bias_rows)
    bias_2 = bias_rows - bias_1
    bias_terms = jnp.concatenate(
        [
            jnp.concatenate([bias_1, bias_1], axis=1),
            jnp.concatenate([bias_2, bias_2], axis=1),
        ],
        axis=0,
    ).astype(jnp.bfloat16)
    chain_column = column_of(chain_weight[...], slots)
    chains = key_chain[...]

    loads[14].wait()
    change = dot_nn(right_terms, mixer_terms)
    for row in range(rows):
        slab, place = row // slab_rows, row % slab_rows
        updated = pair[slab, place] + change[:, row * channels : (row + 1) * channels]
        fresh[slab, place] = updated
        upper = rounded(updated)
        both = jnp.concatenate([upper, updated - upper], axis=1).astype(jnp.bfloat16)
        logits = dot_nt(bias_terms, both)
        differ = (chains != query_chain[slab, place]).astype(jnp.float32)
        bias[slab, place] = logits[:slots] + logits[slots:] + chain_column * differ

    store = pltpu.make_async_copy(fresh, new_pair_hbm, store_sem)
    store.start()

    for copy in q_copies:
        copy.wait()
    half = cols // 2
    query = jnp.concatenate(
        [parts_q[place].astype(jnp.float32) for place in range(half)], axis=1
    )
    gate = jax.nn.sigmoid(
        jnp.concatenate(
            [parts_q[place].astype(jnp.float32) for place in range(half, cols)], axis=1
        )
    )
    for place in range(cols):
        gates[place] = gate[place * own_rows : (place + 1) * own_rows]
    on_head = iota((rows, slots, width), 2) // head_width == iota((rows, slots, width), 1)
    query_blocks = (
        jnp.where(on_head, query[:, None, :], 0.0)
        .reshape(rows * slots, width)
        .astype(jnp.bfloat16)
    )
    kv_copy.wait()
    scores = dot_nt(query_blocks, keys_values[0]) * (1.0 / math.sqrt(head_width)) + bias[
        ...
    ].reshape(rows * slots, keys)
    maxima = jnp.max(scores, axis=1, keepdims=True)
    exponent = jnp.exp(scores - maxima)
    totals = jnp.sum(exponent, axis=1, keepdims=True)
    summed = dot_nn(exponent.astype(jnp.bfloat16), keys_values[1]).reshape(rows, slots, width)
    summed = jnp.sum(jnp.where(on_head, summed, 0.0), axis=1)
    on_lane = iota((rows, slots, LANES), 2) == iota((rows, slots, LANES), 1)

    def by_lane(column):
        return jnp.sum(jnp.where(on_lane, column.reshape(rows, slots, 1), 0.0), axis=1)

    bundle = jnp.concatenate([summed, by_lane(maxima), by_lane(totals)], axis=1)
    for place in range(cols):
        packed[place] = bundle[place * own_rows : (place + 1) * own_rows]
    p_copies = [
        pltpu.make_async_remote_copy(
            src_ref=packed.at[peer], dst_ref=partial.at[me],
            send_sem=p_send.at[place], recv_sem=p_recv.at[place],
            device_id={"col": peer}, device_id_type=pl.DeviceIdType.MESH,
        )
        for place, peer in enumerate(peers)
    ]
    for copy in p_copies:
        copy.start()
    partial[me] = packed[me]
    gate_own = gates[me]
    spread_heads = (
        (iota((LANES, width), 1) // head_width == iota((LANES, width), 0))
        .astype(jnp.float32)
    )
    loads[15].wait()
    for copy in p_copies:
        copy.wait()

    maxima = [partial[place, :, width : width + LANES] for place in range(cols)]
    totals = [partial[place, :, width + LANES :] for place in range(cols)]
    peak = functools.reduce(jnp.maximum, maxima)
    scales = [jnp.exp(part - peak) for part in maxima]
    total = functools.reduce(jnp.add, [a * b for a, b in zip(totals, scales)])
    total = jnp.where(iota(total.shape, 1) < heads, total, 1.0)
    shares = dot_nn(
        jnp.concatenate([scale / total for scale in scales], axis=0), spread_heads, HIGHEST
    )
    joint = functools.reduce(
        jnp.add,
        [
            shares[place * own_rows : (place + 1) * own_rows] * partial[place, :, :width]
            for place in range(cols)
        ],
    )
    attended = joint * gate_own
    attended = jnp.concatenate(
        [attended, jnp.zeros((rows - own_rows, width), jnp.float32)], axis=0
    ).astype(jnp.bfloat16)

    final[me] = rounded(dot_nn(attended, out_proj[...])[:own_rows])
    f_copies = [
        pltpu.make_async_remote_copy(
            src_ref=final.at[me], dst_ref=final.at[me],
            send_sem=f_send.at[place], recv_sem=f_recv.at[place],
            device_id={"col": peer}, device_id_type=pl.DeviceIdType.MESH,
        )
        for place, peer in enumerate(peers)
    ]
    for copy in f_copies:
        copy.start()
    store.wait()
    for copy in f_copies:
        copy.wait()
    single_update[...] = (
        jnp.concatenate([final[place] for place in range(cols)], axis=0)
        .reshape(slabs, slab_rows, width)
        .astype(jnp.bfloat16)
    )


LANES = 128
OPERANDS = 16


def fused(
    pair_block, query_single, key_single, query_chain, key_chain, query_mask, key_mask,
    timestep, time_table, norm_gain, left_proj, right_proj, outer_proj, bias_proj,
    chain_weight, query_proj, kv_proj, out_proj,
):
    cols = lax.axis_size("col")
    slabs, slab_rows, width = query_single.shape
    rows = slabs * slab_rows
    keys = key_single.shape[0]
    heads = chain_weight.shape[0]
    slots = -(-heads // 16) * 16
    own_rows = rows // cols
    operands = (
        time_table, query_single, query_mask, norm_gain.reshape(-1, LANES), query_proj.T,
        key_single, key_mask.reshape(1, -1), kv_proj, left_proj.T, right_proj.T, outer_proj,
        bias_proj.T, chain_weight.reshape(1, -1), key_chain.reshape(1, -1), pair_block, out_proj,
    )
    smem = pl.BlockSpec(memory_space=pltpu.SMEM)
    far = pl.BlockSpec(memory_space=pltpu.HBM)
    dma = pltpu.SemaphoreType.DMA
    return pl.pallas_call(
        fused_kernel,
        out_shape=(
            jax.ShapeDtypeStruct(pair_block.shape, jnp.float32),
            jax.ShapeDtypeStruct(query_single.shape, jnp.bfloat16),
        ),
        in_specs=[smem, smem] + [far] * len(operands),
        out_specs=(far, pl.BlockSpec(memory_space=pltpu.VMEM)),
        scratch_shapes=[pltpu.VMEM(operand.shape, operand.dtype) for operand in operands]
        + [
            pltpu.VMEM(pair_block.shape, jnp.float32),
            pltpu.VMEM((cols, rows, query_proj.shape[1]), jnp.bfloat16),
            pltpu.VMEM((2, keys, width), jnp.bfloat16),
            pltpu.VMEM((slabs, slab_rows, slots, keys), jnp.float32),
            pltpu.VMEM((cols, own_rows, width + 2 * LANES), jnp.float32),
            pltpu.VMEM((cols, own_rows, width + 2 * LANES), jnp.float32),
            pltpu.VMEM((cols, own_rows, width), jnp.float32),
            pltpu.VMEM((cols, own_rows, width), jnp.float32),
            dma((len(operands),)),
            dma,
            dma((cols - 1,)),
            dma((cols - 1,)),
            dma,
            dma,
            dma((cols - 1,)),
            dma((cols - 1,)),
            dma((cols - 1,)),
            dma((cols - 1,)),
        ],
        compiler_params=pltpu.CompilerParams(
            collective_id=0, has_side_effects=True, vmem_limit_bytes=60 * 1024 * 1024
        ),
    )(query_chain, timestep, *operands)


def serve(*arrays):
    query_single, chain_weight, kv_proj = arrays[1], arrays[14], arrays[16]
    rows = query_single.shape[0] * query_single.shape[1]
    cols = lax.axis_size("col")
    fits = (
        rows % cols == 0
        and cols % 2 == 0
        and lax.axis_size("row") == 2
        and kv_proj.shape[1] == query_single.shape[2]
        and chain_weight.shape[0] <= LANES
        and query_single.shape[2] % LANES == 0
    )
    return fused(*arrays) if fits else on_device(*arrays)


def solution(mesh):
    return jax.shard_map(
        serve,
        mesh=mesh,
        in_specs=(
            P("grp", "row", "col", None),
            P("grp", "row", None),
            P(("grp", "col"), None),
            P("grp", "row"),
            P(("grp", "col")),
            P("grp", "row"),
            P(("grp", "col")),
            P("grp"),
            P(),
            P(),
            P(),
            P(),
            P(),
            P(),
            P(),
            P(None, "col"),
            P(None, "row"),
            P(),
        ),
        out_specs=(P("grp", "row", "col", None), P("grp", "row", None)),
        check_vma=False,
    )
```

```python
import functools
import math

import jax
import jax.numpy as jnp
from jax import lax
from jax.experimental import pallas as pl
from jax.experimental.pallas import tpu as pltpu
from jax.sharding import PartitionSpec as P

EPSILON = 1e-05
HIGHEST = lax.Precision.HIGHEST


def combined_all(part, axis, combine):
    gathered = jax.tree.map(lambda a: lax.all_gather(a, axis), part)

    def take(source):
        return jax.tree.map(lambda a: lax.dynamic_index_in_dim(a, source, 0, False), gathered)

    return lax.fori_loop(
        1, lax.axis_size(axis), lambda source, state: combine(state, take(source)), take(0)
    )


def normalize(features, norm_gain):
    average = jnp.mean(features, axis=-1, keepdims=True)
    centred = features - average
    spread = jnp.mean(centred * centred, axis=-1, keepdims=True)
    return (centred * lax.rsqrt(spread + EPSILON) * norm_gain).astype(jnp.bfloat16)


def flat_dot(left, right):
    flat_left = left.reshape(-1, left.shape[-1])
    product = jnp.dot(flat_left, right, preferred_element_type=jnp.float32)
    return product.reshape(left.shape[:-1] + (right.shape[-1],))


def combine_parts(former, latter):
    peak_former, total_former, summed_former = former
    peak_latter, total_latter, summed_latter = latter
    peak_joint = jnp.maximum(peak_former, peak_latter)
    scale_former = jnp.exp(peak_former - peak_joint)
    scale_latter = jnp.exp(peak_latter - peak_joint)
    head_width = summed_former.shape[-1] // peak_joint.shape[-1]
    total_joint = total_former * scale_former + total_latter * scale_latter
    summed_joint = summed_former * jnp.repeat(
        scale_former, head_width, axis=-1
    ) + summed_latter * jnp.repeat(scale_latter, head_width, axis=-1)
    return (peak_joint, total_joint, summed_joint)


def local_parts(query_heads, key_heads, value_heads, logit_bias):
    scores = (
        jnp.einsum("srhd,jhd->srhj", query_heads, key_heads, preferred_element_type=jnp.float32)
        * (1.0 / math.sqrt(query_heads.shape[-1]))
        + logit_bias
    )
    maxima = jnp.max(scores, axis=-1)
    exponent = jnp.exp(scores - maxima[..., None])
    totals = jnp.sum(exponent, axis=-1)
    summed = jnp.einsum(
        "srhj,jhd->srhd",
        exponent.astype(jnp.bfloat16),
        value_heads,
        preferred_element_type=jnp.float32,
    )
    return (maxima, totals, summed.reshape(summed.shape[0], summed.shape[1], -1))


def finish(partials, gate_factor, out_proj, heads):
    maxima, totals, summed = combined_all(partials, "col", combine_parts)
    head_width = summed.shape[-1] // heads
    attended = (summed / jnp.repeat(totals, head_width, axis=-1) * gate_factor).astype(jnp.bfloat16)
    return flat_dot(attended, out_proj).astype(jnp.bfloat16)


def on_device(
    pair_block,
    query_single,
    key_single,
    query_chain,
    key_chain,
    query_mask,
    key_mask,
    timestep,
    time_table,
    norm_gain,
    left_proj,
    right_proj,
    outer_proj,
    bias_proj,
    chain_weight,
    query_proj,
    kv_proj,
    out_proj,
):
    step_count = time_table.shape[0]
    picked = jnp.arange(step_count, dtype=jnp.int32) == timestep[0]
    time_row = jnp.sum(
        jnp.where(picked[:, None], time_table.astype(jnp.float32), jnp.float32(0.0)), axis=0
    )
    query_norm = normalize(
        query_single.astype(jnp.float32) + query_mask[:, :, None].astype(jnp.float32) * time_row,
        norm_gain,
    )
    key_norm = normalize(
        key_single.astype(jnp.float32) + key_mask[:, None].astype(jnp.float32) * time_row, norm_gain
    )
    query_part = flat_dot(query_norm, query_proj).astype(jnp.bfloat16)
    query_gate = lax.all_gather(query_part, "col", axis=2, tiled=True)
    half_projected = jnp.dot(key_norm, kv_proj, preferred_element_type=jnp.float32).astype(
        jnp.bfloat16
    )
    keys_values = lax.all_gather(half_projected, "row", axis=1, tiled=True)
    rank = left_proj.shape[1]
    channels = outer_proj.shape[1]
    left_factor = flat_dot(query_norm, left_proj)
    right_factor = jnp.dot(key_norm, right_proj, preferred_element_type=jnp.float32)
    mixer = jnp.einsum(
        "sra,abc->srbc",
        left_factor,
        outer_proj.astype(jnp.float32).reshape(rank, rank, channels),
        precision=HIGHEST,
    )
    new_pair = pair_block + jnp.einsum("jb,srbc->srjc", right_factor, mixer, precision=HIGHEST)
    differ = (query_chain[:, :, None] != key_chain[None, None, :]).astype(jnp.float32)
    logit_bias = (
        jnp.einsum("srjc,ch->srhj", new_pair, bias_proj, precision=HIGHEST)
        + chain_weight[None, None, :, None] * differ[:, :, None, :]
    )
    heads = chain_weight.shape[0]
    model_width = query_norm.shape[-1]
    head_size = model_width // heads
    slab_count = query_gate.shape[0]
    slab_rows = query_gate.shape[1]
    key_count = keys_values.shape[0]
    query_heads = query_gate[:, :, :model_width].reshape(slab_count, slab_rows, heads, head_size)
    gate_factor = jax.nn.sigmoid(query_gate[:, :, model_width:].astype(jnp.float32))
    key_heads = keys_values[:, :model_width].reshape(key_count, heads, head_size)
    value_heads = keys_values[:, model_width:].reshape(key_count, heads, head_size)
    single_update = finish(
        local_parts(query_heads, key_heads, value_heads, logit_bias), gate_factor, out_proj, heads
    )
    return (new_pair, single_update)


def iota(shape, axis):
    return lax.broadcasted_iota(jnp.int32, shape, axis)


def dot_nt(left, right, precision=None):
    return lax.dot_general(
        left, right, (((1,), (1,)), ((), ())), precision=precision,
        preferred_element_type=jnp.float32,
    )


def dot_nn(left, right, precision=None):
    return jnp.dot(left, right, precision=precision, preferred_element_type=jnp.float32)


def rounded(value):
    return value.astype(jnp.bfloat16).astype(jnp.float32)


def column_of(row, count):
    spot = iota((count, row.shape[1]), 0) == iota((count, row.shape[1]), 1)
    return jnp.sum(jnp.where(spot, row, jnp.zeros_like(row)), axis=1, keepdims=True)


def fused_kernel(
    query_chain, timestep, *operands_results_scratch
):
    sources = operands_results_scratch[:OPERANDS]
    new_pair_hbm, single_update = operands_results_scratch[OPERANDS : OPERANDS + 2]
    targets = operands_results_scratch[OPERANDS + 2 : 2 * OPERANDS + 2]
    (
        time_table, query_single, query_mask, norm_gain, query_proj, key_single, key_mask,
        kv_proj, left_proj, right_proj, outer_proj, bias_proj, chain_weight, key_chain, pair,
        out_proj,
    ) = targets
    (
        fresh, parts_q, keys_values, bias, packed, partial, gates, final,
        load_sem, store_sem, q_send, q_recv, kv_send, kv_recv, p_send, p_recv, f_send, f_recv,
    ) = operands_results_scratch[2 * OPERANDS + 2 :]
    cols = lax.axis_size("col")
    me = lax.axis_index("col")
    side = lax.axis_index("row")
    peers = [lax.rem(me + offset, cols) for offset in range(1, cols)]

    loads = [
        pltpu.make_async_copy(source, target, load_sem.at[place])
        for place, (source, target) in enumerate(zip(sources, targets))
    ]
    for load in loads:
        load.start()

    barrier = pltpu.get_barrier_semaphore()
    for peer in peers:
        pl.semaphore_signal(
            barrier, inc=1, device_id={"col": peer}, device_id_type=pl.DeviceIdType.MESH
        )
    pl.semaphore_signal(
        barrier, inc=1, device_id={"row": 1 - side}, device_id_type=pl.DeviceIdType.MESH
    )

    slabs, slab_rows, width = query_single.shape
    rows = slabs * slab_rows
    keys = key_single.shape[0]
    steps = time_table.shape[0]
    rank = left_proj.shape[0]
    channels = outer_proj.shape[1]
    heads = chain_weight.shape[1]
    head_width = width // heads
    slots = bias.shape[2]
    own_rows = rows // cols

    for load in loads[:4]:
        load.wait()
    gain = jnp.concatenate(
        [norm_gain[place : place + 1] for place in range(norm_gain.shape[0])], axis=1
    )

    def normal(features):
        average = jnp.mean(features, axis=-1, keepdims=True)
        centred = features - average
        spread = jnp.mean(centred * centred, axis=-1, keepdims=True)
        return (centred * lax.rsqrt(spread + EPSILON) * gain).astype(jnp.bfloat16)

    picked = iota((steps, width), 0) == timestep[0]
    time_row = jnp.sum(
        jnp.where(picked, time_table[...].astype(jnp.float32), 0.0), axis=0, keepdims=True
    )

    query_flags = jnp.concatenate(
        [
            column_of(query_mask[slab : slab + 1, :].astype(jnp.float32), slab_rows)
            for slab in range(slabs)
        ],
        axis=0,
    )
    query_norm = normal(
        query_single[...].astype(jnp.float32).reshape(rows, width) + query_flags * time_row
    )
    loads[4].wait()
    parts_q[me] = dot_nt(query_norm, query_proj[...]).astype(jnp.bfloat16)

    pl.semaphore_wait(barrier, cols)
    q_copies = [
        pltpu.make_async_remote_copy(
            src_ref=parts_q.at[me], dst_ref=parts_q.at[me],
            send_sem=q_send.at[place], recv_sem=q_recv.at[place],
            device_id={"col": peer}, device_id_type=pl.DeviceIdType.MESH,
        )
        for place, peer in enumerate(peers)
    ]
    for copy in q_copies:
        copy.start()

    loads[5].wait()
    loads[6].wait()
    key_flags = column_of(key_mask[...].astype(jnp.float32), keys)
    key_norm = normal(key_single[...].astype(jnp.float32) + key_flags * time_row)
    loads[7].wait()
    keys_values[side] = dot_nn(key_norm, kv_proj[...]).astype(jnp.bfloat16)
    kv_copy = pltpu.make_async_remote_copy(
        src_ref=keys_values.at[side], dst_ref=keys_values.at[side],
        send_sem=kv_send, recv_sem=kv_recv,
        device_id={"row": 1 - side}, device_id_type=pl.DeviceIdType.MESH,
    )
    kv_copy.start()

    for load in loads[8:14]:
        load.wait()
    square = rank * rank
    terms = 6
    spread_left = iota((square, rank), 0) // rank == iota((square, rank), 1)
    left_spread = dot_nn(spread_left.astype(jnp.bfloat16), left_proj[...]).astype(jnp.bfloat16)
    tile_right = iota((terms * rank, rank), 0) % rank == iota((terms * rank, rank), 1)
    right_tiled = dot_nn(tile_right.astype(jnp.bfloat16), right_proj[...]).astype(jnp.bfloat16)
    left_wide = dot_nt(query_norm, left_spread)
    right_wide = dot_nt(key_norm, right_tiled)
    on_rank = iota((rows, rank, square), 2) % rank == iota((rows, rank, square), 1)
    left_blocks = jnp.where(on_rank, left_wide[:, None, :], 0.0).reshape(rows * rank, square)
    left_1 = rounded(left_blocks)
    left_2 = rounded(left_blocks - left_1)
    left_3 = left_blocks - left_1 - left_2
    mixer = dot_nn(
        jnp.concatenate([left_1, left_2, left_3], axis=1).astype(jnp.bfloat16),
        jnp.concatenate([outer_proj[...]] * 3, axis=0),
    )
    mixer = jnp.concatenate(
        [mixer[row * rank : (row + 1) * rank] for row in range(rows)], axis=1
    )

    right_1 = rounded(right_wide)
    right_2 = rounded(right_wide - right_1)
    right_3 = right_wide - right_1 - right_2
    group = iota(right_wide.shape, 1) // rank
    right_terms = jnp.where(
        group < 3, right_1, jnp.where(group < 5, right_2, right_3)
    ).astype(jnp.bfloat16)
    mixer_1 = rounded(mixer)
    mixer_2 = rounded(mixer - mixer_1)
    mixer_3 = mixer - mixer_1 - mixer_2
    mixer_terms = jnp.concatenate(
        [mixer_1, mixer_2, mixer_3, mixer_1, mixer_2, mixer_1], axis=0
    ).astype(jnp.bfloat16)

    head_spot = (iota((slots, heads), 0) == iota((slots, heads), 1)).astype(jnp.float32)
    bias_rows = dot_nn(head_spot, bias_proj[...], HIGHEST)
    bias_1 = rounded(bias_rows)
    bias_2 = bias_rows - bias_1
    bias_terms = jnp.concatenate(
        [
            jnp.concatenate([bias_1, bias_1], axis=1),
            jnp.concatenate([bias_2, bias_2], axis=1),
        ],
        axis=0,
    ).astype(jnp.bfloat16)
    chain_column = column_of(chain_weight[...], slots)
    chains = key_chain[...]

    loads[14].wait()
    change = dot_nn(right_terms, mixer_terms)
    for row in range(rows):
        slab, place = row // slab_rows, row % slab_rows
        updated = pair[slab, place] + change[:, row * channels : (row + 1) * channels]
        fresh[slab, place] = updated
        upper = rounded(updated)
        both = jnp.concatenate([upper, updated - upper], axis=1).astype(jnp.bfloat16)
        logits = dot_nt(bias_terms, both)
        differ = (chains != query_chain[slab, place]).astype(jnp.float32)
        bias[slab, place] = logits[:slots] + logits[slots:] + chain_column * differ

    store = pltpu.make_async_copy(fresh, new_pair_hbm, store_sem)
    store.start()

    for copy in q_copies:
        copy.wait()
    half = cols // 2
    query = jnp.concatenate(
        [parts_q[place].astype(jnp.float32) for place in range(half)], axis=1
    )
    gate = jax.nn.sigmoid(
        jnp.concatenate(
            [parts_q[place].astype(jnp.float32) for place in range(half, cols)], axis=1
        )
    )
    for place in range(cols):
        gates[place] = gate[place * own_rows : (place + 1) * own_rows]
    on_head = (
        iota((1, slots, width), 2) // head_width == iota((1, slots, width), 1)
    ).astype(jnp.float32)
    query_blocks = (
        (on_head * query[:, None, :])
        .reshape(rows * slots, width)
        .astype(jnp.bfloat16)
    )
    kv_copy.wait()
    scores = dot_nt(query_blocks, keys_values[0]) * (1.0 / math.sqrt(head_width)) + bias[
        ...
    ].reshape(rows * slots, keys)
    maxima = jnp.max(scores, axis=1, keepdims=True)
    exponent = jnp.exp(scores - maxima)
    totals = jnp.sum(exponent, axis=1, keepdims=True)
    summed = dot_nn(exponent.astype(jnp.bfloat16), keys_values[1]).reshape(rows, slots, width)
    summed = jnp.sum(on_head * summed, axis=1)
    on_lane = (iota((1, slots, LANES), 2) == iota((1, slots, LANES), 1)).astype(jnp.float32)

    def by_lane(column):
        return jnp.sum(on_lane * column.reshape(rows, slots, 1), axis=1)

    bundle = jnp.concatenate([summed, by_lane(maxima), by_lane(totals)], axis=1)
    for place in range(cols):
        packed[place] = bundle[place * own_rows : (place + 1) * own_rows]
    p_copies = [
        pltpu.make_async_remote_copy(
            src_ref=packed.at[peer], dst_ref=partial.at[me],
            send_sem=p_send.at[place], recv_sem=p_recv.at[place],
            device_id={"col": peer}, device_id_type=pl.DeviceIdType.MESH,
        )
        for place, peer in enumerate(peers)
    ]
    for copy in p_copies:
        copy.start()
    partial[me] = packed[me]
    gate_own = gates[me]
    spread_heads = (
        iota((2 * LANES, width), 1) // head_width == iota((2 * LANES, width), 0) % LANES
    ).astype(jnp.bfloat16)
    loads[15].wait()
    for copy in p_copies:
        copy.wait()

    maxima = [partial[place, :, width : width + LANES] for place in range(cols)]
    totals = [partial[place, :, width + LANES :] for place in range(cols)]
    peak = functools.reduce(jnp.maximum, maxima)
    scales = [jnp.exp(part - peak) for part in maxima]
    total = functools.reduce(jnp.add, [a * b for a, b in zip(totals, scales)])
    total = jnp.where(iota(total.shape, 1) < heads, total, 1.0)
    share = jnp.concatenate([scale / total for scale in scales], axis=0)
    upper = rounded(share)
    shares = dot_nn(
        jnp.concatenate([upper, share - upper], axis=1).astype(jnp.bfloat16), spread_heads
    )
    joint = functools.reduce(
        jnp.add,
        [
            shares[place * own_rows : (place + 1) * own_rows] * partial[place, :, :width]
            for place in range(cols)
        ],
    )
    attended = joint * gate_own
    attended = jnp.concatenate(
        [attended, jnp.zeros((rows - own_rows, width), jnp.float32)], axis=0
    ).astype(jnp.bfloat16)

    final[me] = rounded(dot_nn(attended, out_proj[...])[:own_rows])
    f_copies = [
        pltpu.make_async_remote_copy(
            src_ref=final.at[me], dst_ref=final.at[me],
            send_sem=f_send.at[place], recv_sem=f_recv.at[place],
            device_id={"col": peer}, device_id_type=pl.DeviceIdType.MESH,
        )
        for place, peer in enumerate(peers)
    ]
    for copy in f_copies:
        copy.start()
    store.wait()
    for copy in f_copies:
        copy.wait()
    single_update[...] = (
        jnp.concatenate([final[place] for place in range(cols)], axis=0)
        .reshape(slabs, slab_rows, width)
        .astype(jnp.bfloat16)
    )


LANES = 128
OPERANDS = 16
VMEM_BYTES = 60 * 1024 * 1024


def hand_on(pair_in, update_in, pair_out, update_out, pair_sem, update_sem):
    slabs, slab_rows = pair_in.shape[:2]
    copies = [pltpu.make_async_copy(update_in, update_out, update_sem)]
    for slab in range(slabs):
        for row in range(slab_rows):
            copies.append(
                pltpu.make_async_copy(
                    pair_in.at[slab, row], pair_out.at[slab, row], pair_sem.at[slab, row]
                )
            )
    for copy in copies:
        copy.start()
    for copy in copies:
        copy.wait()


def fused(
    pair_block, query_single, key_single, query_chain, key_chain, query_mask, key_mask,
    timestep, time_table, norm_gain, left_proj, right_proj, outer_proj, bias_proj,
    chain_weight, query_proj, kv_proj, out_proj,
):
    cols = lax.axis_size("col")
    slabs, slab_rows, width = query_single.shape
    rows = slabs * slab_rows
    keys = key_single.shape[0]
    heads = chain_weight.shape[0]
    slots = -(-heads // 16) * 16
    own_rows = rows // cols
    operands = (
        time_table, query_single, query_mask, norm_gain.reshape(-1, LANES), query_proj.T,
        key_single, key_mask.reshape(1, -1), kv_proj, left_proj.T, right_proj.T, outer_proj,
        bias_proj.T, chain_weight.reshape(1, -1), key_chain.reshape(1, -1), pair_block, out_proj,
    )
    smem = pl.BlockSpec(memory_space=pltpu.SMEM)
    far = pl.BlockSpec(memory_space=pltpu.HBM)
    dma = pltpu.SemaphoreType.DMA
    results = pl.pallas_call(
        fused_kernel,
        out_shape=(
            jax.ShapeDtypeStruct(pair_block.shape, jnp.float32),
            jax.ShapeDtypeStruct(query_single.shape, jnp.bfloat16),
        ),
        in_specs=[smem, smem] + [far] * len(operands),
        out_specs=(far, pl.BlockSpec(memory_space=pltpu.VMEM)),
        scratch_shapes=[pltpu.VMEM(operand.shape, operand.dtype) for operand in operands]
        + [
            pltpu.VMEM(pair_block.shape, jnp.float32),
            pltpu.VMEM((cols, rows, query_proj.shape[1]), jnp.bfloat16),
            pltpu.VMEM((2, keys, width), jnp.bfloat16),
            pltpu.VMEM((slabs, slab_rows, slots, keys), jnp.float32),
            pltpu.VMEM((cols, own_rows, width + 2 * LANES), jnp.float32),
            pltpu.VMEM((cols, own_rows, width + 2 * LANES), jnp.float32),
            pltpu.VMEM((cols, own_rows, width), jnp.float32),
            pltpu.VMEM((cols, own_rows, width), jnp.float32),
            dma((len(operands),)),
            dma,
            dma((cols - 1,)),
            dma((cols - 1,)),
            dma,
            dma,
            dma((cols - 1,)),
            dma((cols - 1,)),
            dma((cols - 1,)),
            dma((cols - 1,)),
        ],
        compiler_params=pltpu.CompilerParams(
            collective_id=0, has_side_effects=True, vmem_limit_bytes=VMEM_BYTES
        ),
    )(query_chain, timestep, *operands)
    return pl.pallas_call(
        hand_on,
        out_shape=tuple(jax.ShapeDtypeStruct(part.shape, part.dtype) for part in results),
        in_specs=[far, far],
        out_specs=(far, far),
        scratch_shapes=[dma((slabs, slab_rows)), dma],
        compiler_params=pltpu.CompilerParams(vmem_limit_bytes=VMEM_BYTES),
    )(*results)


def serve(*arrays):
    query_single, chain_weight, kv_proj = arrays[1], arrays[14], arrays[16]
    rows = query_single.shape[0] * query_single.shape[1]
    cols = lax.axis_size("col")
    fits = (
        rows % cols == 0
        and cols % 2 == 0
        and lax.axis_size("row") == 2
        and kv_proj.shape[1] == query_single.shape[2]
        and chain_weight.shape[0] <= LANES
        and query_single.shape[2] % LANES == 0
    )
    return fused(*arrays) if fits else on_device(*arrays)


def solution(mesh):
    return jax.shard_map(
        serve,
        mesh=mesh,
        in_specs=(
            P("grp", "row", "col", None),
            P("grp", "row", None),
            P(("grp", "col"), None),
            P("grp", "row"),
            P(("grp", "col")),
            P("grp", "row"),
            P(("grp", "col")),
            P("grp"),
            P(),
            P(),
            P(),
            P(),
            P(),
            P(),
            P(),
            P(None, "col"),
            P(None, "row"),
            P(),
        ),
        out_specs=(P("grp", "row", "col", None), P("grp", "row", None)),
        check_vma=False,
    )
```

```python
import functools
import math

import jax
import jax.numpy as jnp
from jax import lax
from jax.experimental import pallas as pl
from jax.experimental.pallas import tpu as pltpu
from jax.sharding import PartitionSpec as P

EPSILON = 1e-05
HIGHEST = lax.Precision.HIGHEST


def combined_all(part, axis, combine):
    gathered = jax.tree.map(lambda a: lax.all_gather(a, axis), part)

    def take(source):
        return jax.tree.map(lambda a: lax.dynamic_index_in_dim(a, source, 0, False), gathered)

    return lax.fori_loop(
        1, lax.axis_size(axis), lambda source, state: combine(state, take(source)), take(0)
    )


def normalize(features, norm_gain):
    average = jnp.mean(features, axis=-1, keepdims=True)
    centred = features - average
    spread = jnp.mean(centred * centred, axis=-1, keepdims=True)
    return (centred * lax.rsqrt(spread + EPSILON) * norm_gain).astype(jnp.bfloat16)


def flat_dot(left, right):
    flat_left = left.reshape(-1, left.shape[-1])
    product = jnp.dot(flat_left, right, preferred_element_type=jnp.float32)
    return product.reshape(left.shape[:-1] + (right.shape[-1],))


def combine_parts(former, latter):
    peak_former, total_former, summed_former = former
    peak_latter, total_latter, summed_latter = latter
    peak_joint = jnp.maximum(peak_former, peak_latter)
    scale_former = jnp.exp(peak_former - peak_joint)
    scale_latter = jnp.exp(peak_latter - peak_joint)
    head_width = summed_former.shape[-1] // peak_joint.shape[-1]
    total_joint = total_former * scale_former + total_latter * scale_latter
    summed_joint = summed_former * jnp.repeat(
        scale_former, head_width, axis=-1
    ) + summed_latter * jnp.repeat(scale_latter, head_width, axis=-1)
    return (peak_joint, total_joint, summed_joint)


def local_parts(query_heads, key_heads, value_heads, logit_bias):
    scores = (
        jnp.einsum("srhd,jhd->srhj", query_heads, key_heads, preferred_element_type=jnp.float32)
        * (1.0 / math.sqrt(query_heads.shape[-1]))
        + logit_bias
    )
    maxima = jnp.max(scores, axis=-1)
    exponent = jnp.exp(scores - maxima[..., None])
    totals = jnp.sum(exponent, axis=-1)
    summed = jnp.einsum(
        "srhj,jhd->srhd",
        exponent.astype(jnp.bfloat16),
        value_heads,
        preferred_element_type=jnp.float32,
    )
    return (maxima, totals, summed.reshape(summed.shape[0], summed.shape[1], -1))


def finish(partials, gate_factor, out_proj, heads):
    maxima, totals, summed = combined_all(partials, "col", combine_parts)
    head_width = summed.shape[-1] // heads
    attended = (summed / jnp.repeat(totals, head_width, axis=-1) * gate_factor).astype(jnp.bfloat16)
    return flat_dot(attended, out_proj).astype(jnp.bfloat16)


def on_device(
    pair_block,
    query_single,
    key_single,
    query_chain,
    key_chain,
    query_mask,
    key_mask,
    timestep,
    time_table,
    norm_gain,
    left_proj,
    right_proj,
    outer_proj,
    bias_proj,
    chain_weight,
    query_proj,
    kv_proj,
    out_proj,
):
    step_count = time_table.shape[0]
    picked = jnp.arange(step_count, dtype=jnp.int32) == timestep[0]
    time_row = jnp.sum(
        jnp.where(picked[:, None], time_table.astype(jnp.float32), jnp.float32(0.0)), axis=0
    )
    query_norm = normalize(
        query_single.astype(jnp.float32) + query_mask[:, :, None].astype(jnp.float32) * time_row,
        norm_gain,
    )
    key_norm = normalize(
        key_single.astype(jnp.float32) + key_mask[:, None].astype(jnp.float32) * time_row, norm_gain
    )
    query_part = flat_dot(query_norm, query_proj).astype(jnp.bfloat16)
    query_gate = lax.all_gather(query_part, "col", axis=2, tiled=True)
    half_projected = jnp.dot(key_norm, kv_proj, preferred_element_type=jnp.float32).astype(
        jnp.bfloat16
    )
    keys_values = lax.all_gather(half_projected, "row", axis=1, tiled=True)
    rank = left_proj.shape[1]
    channels = outer_proj.shape[1]
    left_factor = flat_dot(query_norm, left_proj)
    right_factor = jnp.dot(key_norm, right_proj, preferred_element_type=jnp.float32)
    mixer = jnp.einsum(
        "sra,abc->srbc",
        left_factor,
        outer_proj.astype(jnp.float32).reshape(rank, rank, channels),
        precision=HIGHEST,
    )
    new_pair = pair_block + jnp.einsum("jb,srbc->srjc", right_factor, mixer, precision=HIGHEST)
    differ = (query_chain[:, :, None] != key_chain[None, None, :]).astype(jnp.float32)
    logit_bias = (
        jnp.einsum("srjc,ch->srhj", new_pair, bias_proj, precision=HIGHEST)
        + chain_weight[None, None, :, None] * differ[:, :, None, :]
    )
    heads = chain_weight.shape[0]
    model_width = query_norm.shape[-1]
    head_size = model_width // heads
    slab_count = query_gate.shape[0]
    slab_rows = query_gate.shape[1]
    key_count = keys_values.shape[0]
    query_heads = query_gate[:, :, :model_width].reshape(slab_count, slab_rows, heads, head_size)
    gate_factor = jax.nn.sigmoid(query_gate[:, :, model_width:].astype(jnp.float32))
    key_heads = keys_values[:, :model_width].reshape(key_count, heads, head_size)
    value_heads = keys_values[:, model_width:].reshape(key_count, heads, head_size)
    single_update = finish(
        local_parts(query_heads, key_heads, value_heads, logit_bias), gate_factor, out_proj, heads
    )
    return (new_pair, single_update)


def iota(shape, axis):
    return lax.broadcasted_iota(jnp.int32, shape, axis)


def dot_nt(left, right, precision=None):
    return lax.dot_general(
        left, right, (((1,), (1,)), ((), ())), precision=precision,
        preferred_element_type=jnp.float32,
    )


def dot_nn(left, right, precision=None):
    return jnp.dot(left, right, precision=precision, preferred_element_type=jnp.float32)


def rounded(value):
    return value.astype(jnp.bfloat16).astype(jnp.float32)


def column_of(row, count):
    spot = iota((count, row.shape[1]), 0) == iota((count, row.shape[1]), 1)
    return jnp.sum(jnp.where(spot, row, jnp.zeros_like(row)), axis=1, keepdims=True)


def fused_kernel(
    query_chain, timestep, *operands_results_scratch
):
    sources = operands_results_scratch[:OPERANDS]
    new_pair, single_update = operands_results_scratch[OPERANDS : OPERANDS + 2]
    targets = operands_results_scratch[OPERANDS + 2 : 2 * OPERANDS + 2]
    (
        time_table, query_single, query_mask, norm_gain, query_proj, key_single, key_mask,
        kv_proj, left_proj, right_proj, outer_proj, bias_proj, chain_weight, key_chain, pair,
        out_proj,
    ) = targets
    (
        parts_q, keys_values, bias, packed, partial, gates, final,
        load_sem, q_send, q_recv, kv_send, kv_recv, p_send, p_recv, f_send, f_recv,
    ) = operands_results_scratch[2 * OPERANDS + 2 :]
    cols = lax.axis_size("col")
    me = lax.axis_index("col")
    side = lax.axis_index("row")
    peers = [lax.rem(me + offset, cols) for offset in range(1, cols)]

    loads = [
        pltpu.make_async_copy(source, target, load_sem.at[place])
        for place, (source, target) in enumerate(zip(sources, targets))
    ]
    for load in loads:
        load.start()

    barrier = pltpu.get_barrier_semaphore()
    for peer in peers:
        pl.semaphore_signal(
            barrier, inc=1, device_id={"col": peer}, device_id_type=pl.DeviceIdType.MESH
        )
    pl.semaphore_signal(
        barrier, inc=1, device_id={"row": 1 - side}, device_id_type=pl.DeviceIdType.MESH
    )

    slabs, slab_rows, width = query_single.shape
    rows = slabs * slab_rows
    keys = key_single.shape[0]
    steps = time_table.shape[0]
    rank = left_proj.shape[0]
    channels = outer_proj.shape[1]
    heads = chain_weight.shape[1]
    head_width = width // heads
    slots = bias.shape[2]
    own_rows = rows // cols

    for load in loads[:4]:
        load.wait()
    gain = jnp.concatenate(
        [norm_gain[place : place + 1] for place in range(norm_gain.shape[0])], axis=1
    )

    def normal(features):
        average = jnp.mean(features, axis=-1, keepdims=True)
        centred = features - average
        spread = jnp.mean(centred * centred, axis=-1, keepdims=True)
        return (centred * lax.rsqrt(spread + EPSILON) * gain).astype(jnp.bfloat16)

    picked = iota((steps, width), 0) == timestep[0]
    time_row = jnp.sum(
        jnp.where(picked, time_table[...].astype(jnp.float32), 0.0), axis=0, keepdims=True
    )

    query_flags = jnp.concatenate(
        [
            column_of(query_mask[slab : slab + 1, :].astype(jnp.float32), slab_rows)
            for slab in range(slabs)
        ],
        axis=0,
    )
    query_norm = normal(
        query_single[...].astype(jnp.float32).reshape(rows, width) + query_flags * time_row
    )
    loads[4].wait()
    parts_q[me] = dot_nt(query_norm, query_proj[...]).astype(jnp.bfloat16)

    pl.semaphore_wait(barrier, cols)
    q_copies = [
        pltpu.make_async_remote_copy(
            src_ref=parts_q.at[me], dst_ref=parts_q.at[me],
            send_sem=q_send.at[place], recv_sem=q_recv.at[place],
            device_id={"col": peer}, device_id_type=pl.DeviceIdType.MESH,
        )
        for place, peer in enumerate(peers)
    ]
    for copy in q_copies:
        copy.start()

    loads[5].wait()
    loads[6].wait()
    key_flags = column_of(key_mask[...].astype(jnp.float32), keys)
    key_norm = normal(key_single[...].astype(jnp.float32) + key_flags * time_row)
    loads[7].wait()
    keys_values[side] = dot_nn(key_norm, kv_proj[...]).astype(jnp.bfloat16)
    kv_copy = pltpu.make_async_remote_copy(
        src_ref=keys_values.at[side], dst_ref=keys_values.at[side],
        send_sem=kv_send, recv_sem=kv_recv,
        device_id={"row": 1 - side}, device_id_type=pl.DeviceIdType.MESH,
    )
    kv_copy.start()

    for load in loads[8:14]:
        load.wait()
    square = rank * rank
    terms = 6
    spread_left = iota((square, rank), 0) // rank == iota((square, rank), 1)
    left_spread = dot_nn(spread_left.astype(jnp.bfloat16), left_proj[...]).astype(jnp.bfloat16)
    tile_right = iota((terms * rank, rank), 0) % rank == iota((terms * rank, rank), 1)
    right_tiled = dot_nn(tile_right.astype(jnp.bfloat16), right_proj[...]).astype(jnp.bfloat16)
    left_wide = dot_nt(query_norm, left_spread)
    right_wide = dot_nt(key_norm, right_tiled)
    on_rank = iota((rows, rank, square), 2) % rank == iota((rows, rank, square), 1)
    left_blocks = jnp.where(on_rank, left_wide[:, None, :], 0.0).reshape(rows * rank, square)
    left_1 = rounded(left_blocks)
    left_2 = rounded(left_blocks - left_1)
    left_3 = left_blocks - left_1 - left_2
    mixer = dot_nn(
        jnp.concatenate([left_1, left_2, left_3], axis=1).astype(jnp.bfloat16),
        jnp.concatenate([outer_proj[...]] * 3, axis=0),
    )
    mixer = jnp.concatenate(
        [mixer[row * rank : (row + 1) * rank] for row in range(rows)], axis=1
    )

    right_1 = rounded(right_wide)
    right_2 = rounded(right_wide - right_1)
    right_3 = right_wide - right_1 - right_2
    group = iota(right_wide.shape, 1) // rank
    right_terms = jnp.where(
        group < 3, right_1, jnp.where(group < 5, right_2, right_3)
    ).astype(jnp.bfloat16)
    mixer_1 = rounded(mixer)
    mixer_2 = rounded(mixer - mixer_1)
    mixer_3 = mixer - mixer_1 - mixer_2
    mixer_terms = jnp.concatenate(
        [mixer_1, mixer_2, mixer_3, mixer_1, mixer_2, mixer_1], axis=0
    ).astype(jnp.bfloat16)

    head_spot = (iota((slots, heads), 0) == iota((slots, heads), 1)).astype(jnp.float32)
    bias_rows = dot_nn(head_spot, bias_proj[...], HIGHEST)
    bias_1 = rounded(bias_rows)
    bias_2 = bias_rows - bias_1
    bias_terms = jnp.concatenate(
        [
            jnp.concatenate([bias_1, bias_1], axis=1),
            jnp.concatenate([bias_2, bias_2], axis=1),
        ],
        axis=0,
    ).astype(jnp.bfloat16)
    chain_column = column_of(chain_weight[...], slots)
    chains = key_chain[...]

    loads[14].wait()
    change = dot_nn(right_terms, mixer_terms)
    for row in range(rows):
        slab, place = row // slab_rows, row % slab_rows
        updated = pair[slab, place] + change[:, row * channels : (row + 1) * channels]
        new_pair[slab, place] = updated
        upper = rounded(updated)
        both = jnp.concatenate([upper, updated - upper], axis=1).astype(jnp.bfloat16)
        logits = dot_nt(bias_terms, both)
        differ = (chains != query_chain[slab, place]).astype(jnp.float32)
        bias[slab, place] = logits[:slots] + logits[slots:] + chain_column * differ


    for copy in q_copies:
        copy.wait()
    half = cols // 2
    query = jnp.concatenate(
        [parts_q[place].astype(jnp.float32) for place in range(half)], axis=1
    )
    gate = jax.nn.sigmoid(
        jnp.concatenate(
            [parts_q[place].astype(jnp.float32) for place in range(half, cols)], axis=1
        )
    )
    for place in range(cols):
        gates[place] = gate[place * own_rows : (place + 1) * own_rows]
    on_head = (
        iota((1, slots, width), 2) // head_width == iota((1, slots, width), 1)
    ).astype(jnp.float32)
    query_blocks = (
        (on_head * query[:, None, :])
        .reshape(rows * slots, width)
        .astype(jnp.bfloat16)
    )
    kv_copy.wait()
    scores = dot_nt(query_blocks, keys_values[0]) * (1.0 / math.sqrt(head_width)) + bias[
        ...
    ].reshape(rows * slots, keys)
    maxima = jnp.max(scores, axis=1, keepdims=True)
    exponent = jnp.exp(scores - maxima)
    totals = jnp.sum(exponent, axis=1, keepdims=True)
    summed = dot_nn(exponent.astype(jnp.bfloat16), keys_values[1]).reshape(rows, slots, width)
    summed = jnp.sum(on_head * summed, axis=1)
    on_lane = (iota((1, slots, LANES), 2) == iota((1, slots, LANES), 1)).astype(jnp.float32)

    def by_lane(column):
        return jnp.sum(on_lane * column.reshape(rows, slots, 1), axis=1)

    bundle = jnp.concatenate([summed, by_lane(maxima), by_lane(totals)], axis=1)
    for place in range(cols):
        packed[place] = bundle[place * own_rows : (place + 1) * own_rows]
    p_copies = [
        pltpu.make_async_remote_copy(
            src_ref=packed.at[peer], dst_ref=partial.at[me],
            send_sem=p_send.at[place], recv_sem=p_recv.at[place],
            device_id={"col": peer}, device_id_type=pl.DeviceIdType.MESH,
        )
        for place, peer in enumerate(peers)
    ]
    for copy in p_copies:
        copy.start()
    partial[me] = packed[me]
    gate_own = gates[me]
    spread_heads = (
        iota((2 * LANES, width), 1) // head_width == iota((2 * LANES, width), 0) % LANES
    ).astype(jnp.bfloat16)
    loads[15].wait()
    for copy in p_copies:
        copy.wait()

    maxima = [partial[place, :, width : width + LANES] for place in range(cols)]
    totals = [partial[place, :, width + LANES :] for place in range(cols)]
    peak = functools.reduce(jnp.maximum, maxima)
    scales = [jnp.exp(part - peak) for part in maxima]
    total = functools.reduce(jnp.add, [a * b for a, b in zip(totals, scales)])
    total = jnp.where(iota(total.shape, 1) < heads, total, 1.0)
    share = jnp.concatenate([scale / total for scale in scales], axis=0)
    upper = rounded(share)
    shares = dot_nn(
        jnp.concatenate([upper, share - upper], axis=1).astype(jnp.bfloat16), spread_heads
    )
    joint = functools.reduce(
        jnp.add,
        [
            shares[place * own_rows : (place + 1) * own_rows] * partial[place, :, :width]
            for place in range(cols)
        ],
    )
    attended = joint * gate_own
    attended = jnp.concatenate(
        [attended, jnp.zeros((rows - own_rows, width), jnp.float32)], axis=0
    ).astype(jnp.bfloat16)

    final[me] = rounded(dot_nn(attended, out_proj[...])[:own_rows])
    f_copies = [
        pltpu.make_async_remote_copy(
            src_ref=final.at[me], dst_ref=final.at[me],
            send_sem=f_send.at[place], recv_sem=f_recv.at[place],
            device_id={"col": peer}, device_id_type=pl.DeviceIdType.MESH,
        )
        for place, peer in enumerate(peers)
    ]
    for copy in f_copies:
        copy.start()
    for copy in f_copies:
        copy.wait()
    single_update[...] = (
        jnp.concatenate([final[place] for place in range(cols)], axis=0)
        .reshape(slabs, slab_rows, width)
        .astype(jnp.bfloat16)
    )


LANES = 128
OPERANDS = 16
VMEM_BYTES = 60 * 1024 * 1024


def hand_on(pair_in, update_in, pair_out, update_out, pair_sem, update_sem):
    slabs = pair_in.shape[0]
    copies = [
        pltpu.make_async_copy(pair_in.at[slab], pair_out.at[slab], pair_sem.at[slab])
        for slab in range(slabs)
    ] + [pltpu.make_async_copy(update_in, update_out, update_sem)]
    for copy in copies:
        copy.start()
    for copy in copies:
        copy.wait()


def fused(
    pair_block, query_single, key_single, query_chain, key_chain, query_mask, key_mask,
    timestep, time_table, norm_gain, left_proj, right_proj, outer_proj, bias_proj,
    chain_weight, query_proj, kv_proj, out_proj,
):
    cols = lax.axis_size("col")
    slabs, slab_rows, width = query_single.shape
    rows = slabs * slab_rows
    keys = key_single.shape[0]
    heads = chain_weight.shape[0]
    slots = -(-heads // 16) * 16
    own_rows = rows // cols
    operands = (
        time_table, query_single, query_mask, norm_gain.reshape(-1, LANES), query_proj.T,
        key_single, key_mask.reshape(1, -1), kv_proj, left_proj.T, right_proj.T, outer_proj,
        bias_proj.T, chain_weight.reshape(1, -1), key_chain.reshape(1, -1), pair_block, out_proj,
    )
    smem = pl.BlockSpec(memory_space=pltpu.SMEM)
    near = pl.BlockSpec(memory_space=pltpu.VMEM)
    far = pl.BlockSpec(memory_space=pltpu.HBM)
    dma = pltpu.SemaphoreType.DMA
    results = pl.pallas_call(
        fused_kernel,
        out_shape=(
            pltpu.VMEM(pair_block.shape, jnp.float32),
            pltpu.VMEM(query_single.shape, jnp.bfloat16),
        ),
        in_specs=[smem, smem] + [far] * len(operands),
        out_specs=(near, near),
        scratch_shapes=[pltpu.VMEM(operand.shape, operand.dtype) for operand in operands]
        + [
            pltpu.VMEM((cols, rows, query_proj.shape[1]), jnp.bfloat16),
            pltpu.VMEM((2, keys, width), jnp.bfloat16),
            pltpu.VMEM((slabs, slab_rows, slots, keys), jnp.float32),
            pltpu.VMEM((cols, own_rows, width + 2 * LANES), jnp.float32),
            pltpu.VMEM((cols, own_rows, width + 2 * LANES), jnp.float32),
            pltpu.VMEM((cols, own_rows, width), jnp.float32),
            pltpu.VMEM((cols, own_rows, width), jnp.float32),
            dma((len(operands),)),
            dma((cols - 1,)),
            dma((cols - 1,)),
            dma,
            dma,
            dma((cols - 1,)),
            dma((cols - 1,)),
            dma((cols - 1,)),
            dma((cols - 1,)),
        ],
        compiler_params=pltpu.CompilerParams(
            collective_id=0, has_side_effects=True, vmem_limit_bytes=VMEM_BYTES
        ),
    )(query_chain, timestep, *operands)
    return pl.pallas_call(
        hand_on,
        out_shape=tuple(jax.ShapeDtypeStruct(part.shape, part.dtype) for part in results),
        in_specs=[near, near],
        out_specs=(far, far),
        scratch_shapes=[dma((slabs,)), dma],
        compiler_params=pltpu.CompilerParams(vmem_limit_bytes=VMEM_BYTES // 60),
    )(*results)


def serve(*arrays):
    query_single, chain_weight, kv_proj = arrays[1], arrays[14], arrays[16]
    rows = query_single.shape[0] * query_single.shape[1]
    cols = lax.axis_size("col")
    fits = (
        rows % cols == 0
        and cols % 2 == 0
        and lax.axis_size("row") == 2
        and kv_proj.shape[1] == query_single.shape[2]
        and chain_weight.shape[0] <= LANES
        and query_single.shape[2] % LANES == 0
    )
    return fused(*arrays) if fits else on_device(*arrays)


def solution(mesh):
    return jax.shard_map(
        serve,
        mesh=mesh,
        in_specs=(
            P("grp", "row", "col", None),
            P("grp", "row", None),
            P(("grp", "col"), None),
            P("grp", "row"),
            P(("grp", "col")),
            P("grp", "row"),
            P(("grp", "col")),
            P("grp"),
            P(),
            P(),
            P(),
            P(),
            P(),
            P(),
            P(),
            P(None, "col"),
            P(None, "row"),
            P(),
        ),
        out_specs=(P("grp", "row", "col", None), P("grp", "row", None)),
        check_vma=False,
    )
```

```python
import functools
import math

import jax
import jax.numpy as jnp
from jax import lax
from jax.experimental import pallas as pl
from jax.experimental.pallas import tpu as pltpu
from jax.sharding import PartitionSpec as P

EPSILON = 1e-05
HIGHEST = lax.Precision.HIGHEST


def combined_all(part, axis, combine):
    gathered = jax.tree.map(lambda a: lax.all_gather(a, axis), part)

    def take(source):
        return jax.tree.map(lambda a: lax.dynamic_index_in_dim(a, source, 0, False), gathered)

    return lax.fori_loop(
        1, lax.axis_size(axis), lambda source, state: combine(state, take(source)), take(0)
    )


def normalize(features, norm_gain):
    average = jnp.mean(features, axis=-1, keepdims=True)
    centred = features - average
    spread = jnp.mean(centred * centred, axis=-1, keepdims=True)
    return (centred * lax.rsqrt(spread + EPSILON) * norm_gain).astype(jnp.bfloat16)


def flat_dot(left, right):
    flat_left = left.reshape(-1, left.shape[-1])
    product = jnp.dot(flat_left, right, preferred_element_type=jnp.float32)
    return product.reshape(left.shape[:-1] + (right.shape[-1],))


def combine_parts(former, latter):
    peak_former, total_former, summed_former = former
    peak_latter, total_latter, summed_latter = latter
    peak_joint = jnp.maximum(peak_former, peak_latter)
    scale_former = jnp.exp(peak_former - peak_joint)
    scale_latter = jnp.exp(peak_latter - peak_joint)
    head_width = summed_former.shape[-1] // peak_joint.shape[-1]
    total_joint = total_former * scale_former + total_latter * scale_latter
    summed_joint = summed_former * jnp.repeat(
        scale_former, head_width, axis=-1
    ) + summed_latter * jnp.repeat(scale_latter, head_width, axis=-1)
    return (peak_joint, total_joint, summed_joint)


def local_parts(query_heads, key_heads, value_heads, logit_bias):
    scores = (
        jnp.einsum("srhd,jhd->srhj", query_heads, key_heads, preferred_element_type=jnp.float32)
        * (1.0 / math.sqrt(query_heads.shape[-1]))
        + logit_bias
    )
    maxima = jnp.max(scores, axis=-1)
    exponent = jnp.exp(scores - maxima[..., None])
    totals = jnp.sum(exponent, axis=-1)
    summed = jnp.einsum(
        "srhj,jhd->srhd",
        exponent.astype(jnp.bfloat16),
        value_heads,
        preferred_element_type=jnp.float32,
    )
    return (maxima, totals, summed.reshape(summed.shape[0], summed.shape[1], -1))


def finish(partials, gate_factor, out_proj, heads):
    maxima, totals, summed = combined_all(partials, "col", combine_parts)
    head_width = summed.shape[-1] // heads
    attended = (summed / jnp.repeat(totals, head_width, axis=-1) * gate_factor).astype(jnp.bfloat16)
    return flat_dot(attended, out_proj).astype(jnp.bfloat16)


def on_device(
    pair_block,
    query_single,
    key_single,
    query_chain,
    key_chain,
    query_mask,
    key_mask,
    timestep,
    time_table,
    norm_gain,
    left_proj,
    right_proj,
    outer_proj,
    bias_proj,
    chain_weight,
    query_proj,
    kv_proj,
    out_proj,
):
    step_count = time_table.shape[0]
    picked = jnp.arange(step_count, dtype=jnp.int32) == timestep[0]
    time_row = jnp.sum(
        jnp.where(picked[:, None], time_table.astype(jnp.float32), jnp.float32(0.0)), axis=0
    )
    query_norm = normalize(
        query_single.astype(jnp.float32) + query_mask[:, :, None].astype(jnp.float32) * time_row,
        norm_gain,
    )
    key_norm = normalize(
        key_single.astype(jnp.float32) + key_mask[:, None].astype(jnp.float32) * time_row, norm_gain
    )
    query_part = flat_dot(query_norm, query_proj).astype(jnp.bfloat16)
    query_gate = lax.all_gather(query_part, "col", axis=2, tiled=True)
    half_projected = jnp.dot(key_norm, kv_proj, preferred_element_type=jnp.float32).astype(
        jnp.bfloat16
    )
    keys_values = lax.all_gather(half_projected, "row", axis=1, tiled=True)
    rank = left_proj.shape[1]
    channels = outer_proj.shape[1]
    left_factor = flat_dot(query_norm, left_proj)
    right_factor = jnp.dot(key_norm, right_proj, preferred_element_type=jnp.float32)
    mixer = jnp.einsum(
        "sra,abc->srbc",
        left_factor,
        outer_proj.astype(jnp.float32).reshape(rank, rank, channels),
        precision=HIGHEST,
    )
    new_pair = pair_block + jnp.einsum("jb,srbc->srjc", right_factor, mixer, precision=HIGHEST)
    differ = (query_chain[:, :, None] != key_chain[None, None, :]).astype(jnp.float32)
    logit_bias = (
        jnp.einsum("srjc,ch->srhj", new_pair, bias_proj, precision=HIGHEST)
        + chain_weight[None, None, :, None] * differ[:, :, None, :]
    )
    heads = chain_weight.shape[0]
    model_width = query_norm.shape[-1]
    head_size = model_width // heads
    slab_count = query_gate.shape[0]
    slab_rows = query_gate.shape[1]
    key_count = keys_values.shape[0]
    query_heads = query_gate[:, :, :model_width].reshape(slab_count, slab_rows, heads, head_size)
    gate_factor = jax.nn.sigmoid(query_gate[:, :, model_width:].astype(jnp.float32))
    key_heads = keys_values[:, :model_width].reshape(key_count, heads, head_size)
    value_heads = keys_values[:, model_width:].reshape(key_count, heads, head_size)
    single_update = finish(
        local_parts(query_heads, key_heads, value_heads, logit_bias), gate_factor, out_proj, heads
    )
    return (new_pair, single_update)


def iota(shape, axis):
    return lax.broadcasted_iota(jnp.int32, shape, axis)


def dot_nt(left, right, precision=None):
    return lax.dot_general(
        left, right, (((1,), (1,)), ((), ())), precision=precision,
        preferred_element_type=jnp.float32,
    )


def dot_nn(left, right, precision=None):
    return jnp.dot(left, right, precision=precision, preferred_element_type=jnp.float32)


def rounded(value):
    return value.astype(jnp.bfloat16).astype(jnp.float32)


def column_of(row, count):
    spot = iota((count, row.shape[1]), 0) == iota((count, row.shape[1]), 1)
    return jnp.sum(jnp.where(spot, row, jnp.zeros_like(row)), axis=1, keepdims=True)


def fused_kernel(
    query_chain, timestep, *operands_results_scratch
):
    sources = operands_results_scratch[:OPERANDS]
    new_pair, single_update = operands_results_scratch[OPERANDS : OPERANDS + 2]
    targets = operands_results_scratch[OPERANDS + 2 : 2 * OPERANDS + 2]
    (
        time_table, query_single, query_mask, norm_gain, query_proj, key_single, key_mask,
        kv_proj, left_proj, right_proj, outer_proj, bias_proj, chain_weight, key_chain, pair,
        out_proj,
    ) = targets
    (
        parts_q, keys_values, bias, packed, partial, gates, final,
        load_sem, q_send, q_recv, kv_send, kv_recv, p_send, p_recv, f_send, f_recv,
    ) = operands_results_scratch[2 * OPERANDS + 2 :]
    cols = lax.axis_size("col")
    me = lax.axis_index("col")
    side = lax.axis_index("row")
    peers = [lax.rem(me + offset, cols) for offset in range(1, cols)]

    loads = [
        pltpu.make_async_copy(source, target, load_sem.at[place])
        for place, (source, target) in enumerate(zip(sources, targets))
    ]
    for load in loads:
        load.start()

    barrier = pltpu.get_barrier_semaphore()
    for peer in peers:
        pl.semaphore_signal(
            barrier, inc=1, device_id={"col": peer}, device_id_type=pl.DeviceIdType.MESH
        )
    pl.semaphore_signal(
        barrier, inc=1, device_id={"row": 1 - side}, device_id_type=pl.DeviceIdType.MESH
    )

    slabs, slab_rows, width = query_single.shape
    rows = slabs * slab_rows
    keys = key_single.shape[0]
    steps = time_table.shape[0]
    rank = left_proj.shape[0]
    channels = outer_proj.shape[1]
    heads = chain_weight.shape[1]
    head_width = width // heads
    slots = bias.shape[2]
    own_rows = rows // cols

    for load in loads[:4]:
        load.wait()
    gain = jnp.concatenate(
        [norm_gain[place : place + 1] for place in range(norm_gain.shape[0])], axis=1
    )

    def normal(features):
        average = jnp.mean(features, axis=-1, keepdims=True)
        centred = features - average
        spread = jnp.mean(centred * centred, axis=-1, keepdims=True)
        return (centred * lax.rsqrt(spread + EPSILON) * gain).astype(jnp.bfloat16)

    picked = iota((steps, width), 0) == timestep[0]
    time_row = jnp.sum(
        jnp.where(picked, time_table[...].astype(jnp.float32), 0.0), axis=0, keepdims=True
    )

    query_flags = jnp.concatenate(
        [
            column_of(query_mask[slab : slab + 1, :].astype(jnp.float32), slab_rows)
            for slab in range(slabs)
        ],
        axis=0,
    )
    query_norm = normal(
        query_single[...].astype(jnp.float32).reshape(rows, width) + query_flags * time_row
    )
    loads[4].wait()
    parts_q[me] = dot_nt(query_norm, query_proj[...]).astype(jnp.bfloat16)

    pl.semaphore_wait(barrier, cols)
    q_copies = [
        pltpu.make_async_remote_copy(
            src_ref=parts_q.at[me], dst_ref=parts_q.at[me],
            send_sem=q_send.at[place], recv_sem=q_recv.at[place],
            device_id={"col": peer}, device_id_type=pl.DeviceIdType.MESH,
        )
        for place, peer in enumerate(peers)
    ]
    for copy in q_copies:
        copy.start()

    loads[5].wait()
    loads[6].wait()
    key_flags = column_of(key_mask[...].astype(jnp.float32), keys)
    key_norm = normal(key_single[...].astype(jnp.float32) + key_flags * time_row)
    for load in loads[8:14]:
        load.wait()

    square = rank * rank
    terms = 6
    spread_left = iota((square, rank), 0) // rank == iota((square, rank), 1)
    left_spread = dot_nn(spread_left.astype(jnp.bfloat16), left_proj[...]).astype(jnp.bfloat16)
    tile_right = iota((terms * rank, rank), 0) % rank == iota((terms * rank, rank), 1)
    right_tiled = dot_nn(tile_right.astype(jnp.bfloat16), right_proj[...]).astype(jnp.bfloat16)
    left_wide = dot_nt(query_norm, left_spread)
    on_rank = iota((rows, rank, square), 2) % rank == iota((rows, rank, square), 1)
    left_blocks = jnp.where(on_rank, left_wide[:, None, :], 0.0).reshape(rows * rank, square)
    left_1 = rounded(left_blocks)
    left_2 = rounded(left_blocks - left_1)
    left_3 = left_blocks - left_1 - left_2
    mixer = dot_nn(
        jnp.concatenate([left_1, left_2, left_3], axis=1).astype(jnp.bfloat16),
        jnp.concatenate([outer_proj[...]] * 3, axis=0),
    )
    mixer = jnp.concatenate(
        [mixer[row * rank : (row + 1) * rank] for row in range(rows)], axis=1
    )

    mixer_1 = rounded(mixer)
    mixer_2 = rounded(mixer - mixer_1)
    mixer_3 = mixer - mixer_1 - mixer_2
    mixer_terms = jnp.concatenate(
        [mixer_1, mixer_2, mixer_3, mixer_1, mixer_2, mixer_1], axis=0
    ).astype(jnp.bfloat16)

    head_spot = (iota((slots, heads), 0) == iota((slots, heads), 1)).astype(jnp.float32)
    bias_rows = dot_nn(head_spot, bias_proj[...], HIGHEST)
    bias_1 = rounded(bias_rows)
    bias_2 = bias_rows - bias_1
    bias_terms = jnp.concatenate(
        [
            jnp.concatenate([bias_1, bias_1], axis=1),
            jnp.concatenate([bias_2, bias_2], axis=1),
        ],
        axis=0,
    ).astype(jnp.bfloat16)
    chain_column = column_of(chain_weight[...], slots)
    chains = key_chain[...]


    loads[7].wait()
    projected = dot_nn(key_norm, kv_proj[...]).astype(jnp.bfloat16)
    right_wide = dot_nt(key_norm, right_tiled)
    right_1 = rounded(right_wide)
    right_2 = rounded(right_wide - right_1)
    right_3 = right_wide - right_1 - right_2
    group = iota(right_wide.shape, 1) // rank
    right_terms = jnp.where(
        group < 3, right_1, jnp.where(group < 5, right_2, right_3)
    ).astype(jnp.bfloat16)
    keys_values[side] = projected
    kv_copy = pltpu.make_async_remote_copy(
        src_ref=keys_values.at[side], dst_ref=keys_values.at[side],
        send_sem=kv_send, recv_sem=kv_recv,
        device_id={"row": 1 - side}, device_id_type=pl.DeviceIdType.MESH,
    )
    kv_copy.start()

    loads[14].wait()
    change = dot_nn(right_terms, mixer_terms)
    for row in range(rows):
        slab, place = row // slab_rows, row % slab_rows
        updated = pair[slab, place] + change[:, row * channels : (row + 1) * channels]
        new_pair[slab, place] = updated
        upper = rounded(updated)
        both = jnp.concatenate([upper, updated - upper], axis=1).astype(jnp.bfloat16)
        logits = dot_nt(bias_terms, both)
        differ = (chains != query_chain[slab, place]).astype(jnp.float32)
        bias[slab, place] = logits[:slots] + logits[slots:] + chain_column * differ


    for copy in q_copies:
        copy.wait()
    half = cols // 2
    query = jnp.concatenate(
        [parts_q[place].astype(jnp.float32) for place in range(half)], axis=1
    )
    gate = jax.nn.sigmoid(
        jnp.concatenate(
            [parts_q[place].astype(jnp.float32) for place in range(half, cols)], axis=1
        )
    )
    for place in range(cols):
        gates[place] = gate[place * own_rows : (place + 1) * own_rows]
    on_head = (
        iota((1, slots, width), 2) // head_width == iota((1, slots, width), 1)
    ).astype(jnp.float32)
    query_blocks = (
        (on_head * query[:, None, :])
        .reshape(rows * slots, width)
        .astype(jnp.bfloat16)
    )
    kv_copy.wait()
    scores = dot_nt(query_blocks, keys_values[0]) * (1.0 / math.sqrt(head_width)) + bias[
        ...
    ].reshape(rows * slots, keys)
    maxima = jnp.max(scores, axis=1, keepdims=True)
    exponent = jnp.exp(scores - maxima)
    totals = jnp.sum(exponent, axis=1, keepdims=True)
    summed = dot_nn(exponent.astype(jnp.bfloat16), keys_values[1]).reshape(rows, slots, width)
    summed = jnp.sum(on_head * summed, axis=1)
    on_lane = (iota((1, slots, LANES), 2) == iota((1, slots, LANES), 1)).astype(jnp.float32)

    def by_lane(column):
        return jnp.sum(on_lane * column.reshape(rows, slots, 1), axis=1)

    bundle = jnp.concatenate([summed, by_lane(maxima), by_lane(totals)], axis=1)
    for place in range(cols):
        packed[place] = bundle[place * own_rows : (place + 1) * own_rows]
    p_copies = [
        pltpu.make_async_remote_copy(
            src_ref=packed.at[peer], dst_ref=partial.at[me],
            send_sem=p_send.at[place], recv_sem=p_recv.at[place],
            device_id={"col": peer}, device_id_type=pl.DeviceIdType.MESH,
        )
        for place, peer in enumerate(peers)
    ]
    for copy in p_copies:
        copy.start()
    partial[me] = packed[me]
    gate_own = gates[me]
    spread_heads = (
        iota((2 * LANES, width), 1) // head_width == iota((2 * LANES, width), 0) % LANES
    ).astype(jnp.bfloat16)
    loads[15].wait()
    for copy in p_copies:
        copy.wait()

    maxima = [partial[place, :, width : width + LANES] for place in range(cols)]
    totals = [partial[place, :, width + LANES :] for place in range(cols)]
    peak = functools.reduce(jnp.maximum, maxima)
    scales = [jnp.exp(part - peak) for part in maxima]
    total = functools.reduce(jnp.add, [a * b for a, b in zip(totals, scales)])
    total = jnp.where(iota(total.shape, 1) < heads, total, 1.0)
    share = jnp.concatenate([scale / total for scale in scales], axis=0)
    upper = rounded(share)
    shares = dot_nn(
        jnp.concatenate([upper, share - upper], axis=1).astype(jnp.bfloat16), spread_heads
    )
    joint = functools.reduce(
        jnp.add,
        [
            shares[place * own_rows : (place + 1) * own_rows] * partial[place, :, :width]
            for place in range(cols)
        ],
    )
    attended = joint * gate_own
    attended = jnp.concatenate(
        [attended, jnp.zeros((rows - own_rows, width), jnp.float32)], axis=0
    ).astype(jnp.bfloat16)

    final[me] = rounded(dot_nn(attended, out_proj[...])[:own_rows])
    f_copies = [
        pltpu.make_async_remote_copy(
            src_ref=final.at[me], dst_ref=final.at[me],
            send_sem=f_send.at[place], recv_sem=f_recv.at[place],
            device_id={"col": peer}, device_id_type=pl.DeviceIdType.MESH,
        )
        for place, peer in enumerate(peers)
    ]
    for copy in f_copies:
        copy.start()
    for copy in f_copies:
        copy.wait()
    single_update[...] = (
        jnp.concatenate([final[place] for place in range(cols)], axis=0)
        .reshape(slabs, slab_rows, width)
        .astype(jnp.bfloat16)
    )


LANES = 128
OPERANDS = 16
VMEM_BYTES = 60 * 1024 * 1024


def hand_on(pair_in, update_in, pair_out, update_out, pair_sem, update_sem):
    slabs = pair_in.shape[0]
    copies = [
        pltpu.make_async_copy(pair_in.at[slab], pair_out.at[slab], pair_sem.at[slab])
        for slab in range(slabs)
    ] + [pltpu.make_async_copy(update_in, update_out, update_sem)]
    for copy in copies:
        copy.start()
    for copy in copies:
        copy.wait()


def fused(
    pair_block, query_single, key_single, query_chain, key_chain, query_mask, key_mask,
    timestep, time_table, norm_gain, left_proj, right_proj, outer_proj, bias_proj,
    chain_weight, query_proj, kv_proj, out_proj,
):
    cols = lax.axis_size("col")
    slabs, slab_rows, width = query_single.shape
    rows = slabs * slab_rows
    keys = key_single.shape[0]
    heads = chain_weight.shape[0]
    slots = -(-heads // 16) * 16
    own_rows = rows // cols
    operands = (
        time_table, query_single, query_mask, norm_gain.reshape(-1, LANES), query_proj.T,
        key_single, key_mask.reshape(1, -1), kv_proj, left_proj.T, right_proj.T, outer_proj,
        bias_proj.T, chain_weight.reshape(1, -1), key_chain.reshape(1, -1), pair_block, out_proj,
    )
    smem = pl.BlockSpec(memory_space=pltpu.SMEM)
    near = pl.BlockSpec(memory_space=pltpu.VMEM)
    far = pl.BlockSpec(memory_space=pltpu.HBM)
    dma = pltpu.SemaphoreType.DMA
    results = pl.pallas_call(
        fused_kernel,
        out_shape=(
            pltpu.VMEM(pair_block.shape, jnp.float32),
            pltpu.VMEM(query_single.shape, jnp.bfloat16),
        ),
        in_specs=[smem, smem] + [far] * len(operands),
        out_specs=(near, near),
        scratch_shapes=[pltpu.VMEM(operand.shape, operand.dtype) for operand in operands]
        + [
            pltpu.VMEM((cols, rows, query_proj.shape[1]), jnp.bfloat16),
            pltpu.VMEM((2, keys, width), jnp.bfloat16),
            pltpu.VMEM((slabs, slab_rows, slots, keys), jnp.float32),
            pltpu.VMEM((cols, own_rows, width + 2 * LANES), jnp.float32),
            pltpu.VMEM((cols, own_rows, width + 2 * LANES), jnp.float32),
            pltpu.VMEM((cols, own_rows, width), jnp.float32),
            pltpu.VMEM((cols, own_rows, width), jnp.float32),
            dma((len(operands),)),
            dma((cols - 1,)),
            dma((cols - 1,)),
            dma,
            dma,
            dma((cols - 1,)),
            dma((cols - 1,)),
            dma((cols - 1,)),
            dma((cols - 1,)),
        ],
        compiler_params=pltpu.CompilerParams(
            collective_id=0, has_side_effects=True, vmem_limit_bytes=VMEM_BYTES
        ),
    )(query_chain, timestep, *operands)
    return pl.pallas_call(
        hand_on,
        out_shape=tuple(jax.ShapeDtypeStruct(part.shape, part.dtype) for part in results),
        in_specs=[near, near],
        out_specs=(far, far),
        scratch_shapes=[dma((slabs,)), dma],
        compiler_params=pltpu.CompilerParams(vmem_limit_bytes=VMEM_BYTES // 60),
    )(*results)


def serve(*arrays):
    query_single, chain_weight, kv_proj = arrays[1], arrays[14], arrays[16]
    rows = query_single.shape[0] * query_single.shape[1]
    cols = lax.axis_size("col")
    fits = (
        rows % cols == 0
        and cols % 2 == 0
        and lax.axis_size("row") == 2
        and kv_proj.shape[1] == query_single.shape[2]
        and chain_weight.shape[0] <= LANES
        and query_single.shape[2] % LANES == 0
    )
    return fused(*arrays) if fits else on_device(*arrays)


def solution(mesh):
    return jax.shard_map(
        serve,
        mesh=mesh,
        in_specs=(
            P("grp", "row", "col", None),
            P("grp", "row", None),
            P(("grp", "col"), None),
            P("grp", "row"),
            P(("grp", "col")),
            P("grp", "row"),
            P(("grp", "col")),
            P("grp"),
            P(),
            P(),
            P(),
            P(),
            P(),
            P(),
            P(),
            P(None, "col"),
            P(None, "row"),
            P(),
        ),
        out_specs=(P("grp", "row", "col", None), P("grp", "row", None)),
        check_vma=False,
    )
```

```python
import functools
import math

import jax
import jax.numpy as jnp
from jax import lax
from jax.experimental import pallas as pl
from jax.experimental.pallas import tpu as pltpu
from jax.sharding import PartitionSpec as P

EPSILON = 1e-05
HIGHEST = lax.Precision.HIGHEST


def combined_all(part, axis, combine):
    gathered = jax.tree.map(lambda a: lax.all_gather(a, axis), part)

    def take(source):
        return jax.tree.map(lambda a: lax.dynamic_index_in_dim(a, source, 0, False), gathered)

    return lax.fori_loop(
        1, lax.axis_size(axis), lambda source, state: combine(state, take(source)), take(0)
    )


def normalize(features, norm_gain):
    average = jnp.mean(features, axis=-1, keepdims=True)
    centred = features - average
    spread = jnp.mean(centred * centred, axis=-1, keepdims=True)
    return (centred * lax.rsqrt(spread + EPSILON) * norm_gain).astype(jnp.bfloat16)


def flat_dot(left, right):
    flat_left = left.reshape(-1, left.shape[-1])
    product = jnp.dot(flat_left, right, preferred_element_type=jnp.float32)
    return product.reshape(left.shape[:-1] + (right.shape[-1],))


def combine_parts(former, latter):
    peak_former, total_former, summed_former = former
    peak_latter, total_latter, summed_latter = latter
    peak_joint = jnp.maximum(peak_former, peak_latter)
    scale_former = jnp.exp(peak_former - peak_joint)
    scale_latter = jnp.exp(peak_latter - peak_joint)
    head_width = summed_former.shape[-1] // peak_joint.shape[-1]
    total_joint = total_former * scale_former + total_latter * scale_latter
    summed_joint = summed_former * jnp.repeat(
        scale_former, head_width, axis=-1
    ) + summed_latter * jnp.repeat(scale_latter, head_width, axis=-1)
    return (peak_joint, total_joint, summed_joint)


def local_parts(query_heads, key_heads, value_heads, logit_bias):
    scores = (
        jnp.einsum("srhd,jhd->srhj", query_heads, key_heads, preferred_element_type=jnp.float32)
        * (1.0 / math.sqrt(query_heads.shape[-1]))
        + logit_bias
    )
    maxima = jnp.max(scores, axis=-1)
    exponent = jnp.exp(scores - maxima[..., None])
    totals = jnp.sum(exponent, axis=-1)
    summed = jnp.einsum(
        "srhj,jhd->srhd",
        exponent.astype(jnp.bfloat16),
        value_heads,
        preferred_element_type=jnp.float32,
    )
    return (maxima, totals, summed.reshape(summed.shape[0], summed.shape[1], -1))


def finish(partials, gate_factor, out_proj, heads):
    maxima, totals, summed = combined_all(partials, "col", combine_parts)
    head_width = summed.shape[-1] // heads
    attended = (summed / jnp.repeat(totals, head_width, axis=-1) * gate_factor).astype(jnp.bfloat16)
    return flat_dot(attended, out_proj).astype(jnp.bfloat16)


def on_device(
    pair_block,
    query_single,
    key_single,
    query_chain,
    key_chain,
    query_mask,
    key_mask,
    timestep,
    time_table,
    norm_gain,
    left_proj,
    right_proj,
    outer_proj,
    bias_proj,
    chain_weight,
    query_proj,
    kv_proj,
    out_proj,
):
    step_count = time_table.shape[0]
    picked = jnp.arange(step_count, dtype=jnp.int32) == timestep[0]
    time_row = jnp.sum(
        jnp.where(picked[:, None], time_table.astype(jnp.float32), jnp.float32(0.0)), axis=0
    )
    query_norm = normalize(
        query_single.astype(jnp.float32) + query_mask[:, :, None].astype(jnp.float32) * time_row,
        norm_gain,
    )
    key_norm = normalize(
        key_single.astype(jnp.float32) + key_mask[:, None].astype(jnp.float32) * time_row, norm_gain
    )
    query_part = flat_dot(query_norm, query_proj).astype(jnp.bfloat16)
    query_gate = lax.all_gather(query_part, "col", axis=2, tiled=True)
    half_projected = jnp.dot(key_norm, kv_proj, preferred_element_type=jnp.float32).astype(
        jnp.bfloat16
    )
    keys_values = lax.all_gather(half_projected, "row", axis=1, tiled=True)
    rank = left_proj.shape[1]
    channels = outer_proj.shape[1]
    left_factor = flat_dot(query_norm, left_proj)
    right_factor = jnp.dot(key_norm, right_proj, preferred_element_type=jnp.float32)
    mixer = jnp.einsum(
        "sra,abc->srbc",
        left_factor,
        outer_proj.astype(jnp.float32).reshape(rank, rank, channels),
        precision=HIGHEST,
    )
    new_pair = pair_block + jnp.einsum("jb,srbc->srjc", right_factor, mixer, precision=HIGHEST)
    differ = (query_chain[:, :, None] != key_chain[None, None, :]).astype(jnp.float32)
    logit_bias = (
        jnp.einsum("srjc,ch->srhj", new_pair, bias_proj, precision=HIGHEST)
        + chain_weight[None, None, :, None] * differ[:, :, None, :]
    )
    heads = chain_weight.shape[0]
    model_width = query_norm.shape[-1]
    head_size = model_width // heads
    slab_count = query_gate.shape[0]
    slab_rows = query_gate.shape[1]
    key_count = keys_values.shape[0]
    query_heads = query_gate[:, :, :model_width].reshape(slab_count, slab_rows, heads, head_size)
    gate_factor = jax.nn.sigmoid(query_gate[:, :, model_width:].astype(jnp.float32))
    key_heads = keys_values[:, :model_width].reshape(key_count, heads, head_size)
    value_heads = keys_values[:, model_width:].reshape(key_count, heads, head_size)
    single_update = finish(
        local_parts(query_heads, key_heads, value_heads, logit_bias), gate_factor, out_proj, heads
    )
    return (new_pair, single_update)


def iota(shape, axis):
    return lax.broadcasted_iota(jnp.int32, shape, axis)


def dot_nt(left, right, precision=None):
    return lax.dot_general(
        left, right, (((1,), (1,)), ((), ())), precision=precision,
        preferred_element_type=jnp.float32,
    )


def dot_nn(left, right, precision=None):
    return jnp.dot(left, right, precision=precision, preferred_element_type=jnp.float32)


def rounded(value):
    return value.astype(jnp.bfloat16).astype(jnp.float32)


def column_of(row, count):
    spot = iota((count, row.shape[1]), 0) == iota((count, row.shape[1]), 1)
    return jnp.sum(jnp.where(spot, row, jnp.zeros_like(row)), axis=1, keepdims=True)


class Pieces:
    def __init__(self, source, target, sems):
        count = source.shape[0]
        pieces = PIECES if count % (16 * PIECES) == 0 else 1
        if len(source.shape) == 4:
            pieces = math.gcd(count, PIECES)
        size = count // pieces
        self.copies = [
            pltpu.make_async_copy(
                source.at[pl.ds(piece * size, size)],
                target.at[pl.ds(piece * size, size)],
                sems.at[piece],
            )
            for piece in range(pieces)
        ]

    def start(self):
        for copy in self.copies:
            copy.start()

    def wait(self):
        for copy in self.copies:
            copy.wait()


def fused_kernel(
    query_chain, timestep, *operands_results_scratch
):
    sources = operands_results_scratch[:OPERANDS]
    new_pair, single_update = operands_results_scratch[OPERANDS : OPERANDS + 2]
    targets = operands_results_scratch[OPERANDS + 2 : 2 * OPERANDS + 2]
    (
        time_table, query_single, query_mask, norm_gain, query_proj, key_single, key_mask,
        kv_proj, left_proj, right_proj, outer_proj, bias_proj, chain_weight, key_chain, pair,
        out_proj,
    ) = targets
    (
        parts_q, keys_values, bias, packed, partial, gates, final,
        load_sem, q_send, q_recv, kv_send, kv_recv, p_send, p_recv, f_send, f_recv,
    ) = operands_results_scratch[2 * OPERANDS + 2 :]
    cols = lax.axis_size("col")
    me = lax.axis_index("col")
    side = lax.axis_index("row")
    peers = [lax.rem(me + offset, cols) for offset in range(1, cols)]

    loads = [
        Pieces(source, target, load_sem.at[place])
        for place, (source, target) in enumerate(zip(sources, targets))
    ]
    for load in loads:
        load.start()

    barrier = pltpu.get_barrier_semaphore()
    for peer in peers:
        pl.semaphore_signal(
            barrier, inc=1, device_id={"col": peer}, device_id_type=pl.DeviceIdType.MESH
        )
    pl.semaphore_signal(
        barrier, inc=1, device_id={"row": 1 - side}, device_id_type=pl.DeviceIdType.MESH
    )

    slabs, slab_rows, width = query_single.shape
    rows = slabs * slab_rows
    keys = key_single.shape[0]
    steps = time_table.shape[0]
    rank = left_proj.shape[0]
    channels = outer_proj.shape[1]
    heads = chain_weight.shape[1]
    head_width = width // heads
    slots = bias.shape[2]
    own_rows = rows // cols

    for load in loads[:4]:
        load.wait()
    gain = jnp.concatenate(
        [norm_gain[place : place + 1] for place in range(norm_gain.shape[0])], axis=1
    )

    def normal(features):
        average = jnp.mean(features, axis=-1, keepdims=True)
        centred = features - average
        spread = jnp.mean(centred * centred, axis=-1, keepdims=True)
        return (centred * lax.rsqrt(spread + EPSILON) * gain).astype(jnp.bfloat16)

    picked = iota((steps, width), 0) == timestep[0]
    time_row = jnp.sum(
        jnp.where(picked, time_table[...].astype(jnp.float32), 0.0), axis=0, keepdims=True
    )

    query_flags = jnp.concatenate(
        [
            column_of(query_mask[slab : slab + 1, :].astype(jnp.float32), slab_rows)
            for slab in range(slabs)
        ],
        axis=0,
    )
    query_norm = normal(
        query_single[...].astype(jnp.float32).reshape(rows, width) + query_flags * time_row
    )
    loads[4].wait()
    parts_q[me] = dot_nt(query_norm, query_proj[...]).astype(jnp.bfloat16)

    pl.semaphore_wait(barrier, cols)
    q_copies = [
        pltpu.make_async_remote_copy(
            src_ref=parts_q.at[me], dst_ref=parts_q.at[me],
            send_sem=q_send.at[place], recv_sem=q_recv.at[place],
            device_id={"col": peer}, device_id_type=pl.DeviceIdType.MESH,
        )
        for place, peer in enumerate(peers)
    ]
    for copy in q_copies:
        copy.start()

    loads[5].wait()
    loads[6].wait()
    key_flags = column_of(key_mask[...].astype(jnp.float32), keys)
    key_norm = normal(key_single[...].astype(jnp.float32) + key_flags * time_row)
    for load in loads[8:14]:
        load.wait()

    square = rank * rank
    terms = 6
    spread_left = iota((square, rank), 0) // rank == iota((square, rank), 1)
    left_spread = dot_nn(spread_left.astype(jnp.bfloat16), left_proj[...]).astype(jnp.bfloat16)
    tile_right = iota((terms * rank, rank), 0) % rank == iota((terms * rank, rank), 1)
    right_tiled = dot_nn(tile_right.astype(jnp.bfloat16), right_proj[...]).astype(jnp.bfloat16)
    left_wide = dot_nt(query_norm, left_spread)
    on_rank = iota((rows, rank, square), 2) % rank == iota((rows, rank, square), 1)
    left_blocks = jnp.where(on_rank, left_wide[:, None, :], 0.0).reshape(rows * rank, square)
    left_1 = rounded(left_blocks)
    left_2 = rounded(left_blocks - left_1)
    left_3 = left_blocks - left_1 - left_2
    mixer = dot_nn(
        jnp.concatenate([left_1, left_2, left_3], axis=1).astype(jnp.bfloat16),
        jnp.concatenate([outer_proj[...]] * 3, axis=0),
    )
    mixer = jnp.concatenate(
        [mixer[row * rank : (row + 1) * rank] for row in range(rows)], axis=1
    )

    mixer_1 = rounded(mixer)
    mixer_2 = rounded(mixer - mixer_1)
    mixer_3 = mixer - mixer_1 - mixer_2
    mixer_terms = jnp.concatenate(
        [mixer_1, mixer_2, mixer_3, mixer_1, mixer_2, mixer_1], axis=0
    ).astype(jnp.bfloat16)

    head_spot = (iota((slots, heads), 0) == iota((slots, heads), 1)).astype(jnp.float32)
    bias_rows = dot_nn(head_spot, bias_proj[...], HIGHEST)
    bias_1 = rounded(bias_rows)
    bias_2 = bias_rows - bias_1
    bias_terms = jnp.concatenate(
        [
            jnp.concatenate([bias_1, bias_1], axis=1),
            jnp.concatenate([bias_2, bias_2], axis=1),
        ],
        axis=0,
    ).astype(jnp.bfloat16)
    chain_column = column_of(chain_weight[...], slots)
    chains = key_chain[...]


    loads[7].wait()
    projected = dot_nn(key_norm, kv_proj[...]).astype(jnp.bfloat16)
    right_wide = dot_nt(key_norm, right_tiled)
    right_1 = rounded(right_wide)
    right_2 = rounded(right_wide - right_1)
    right_3 = right_wide - right_1 - right_2
    group = iota(right_wide.shape, 1) // rank
    right_terms = jnp.where(
        group < 3, right_1, jnp.where(group < 5, right_2, right_3)
    ).astype(jnp.bfloat16)
    keys_values[side] = projected
    kv_copy = pltpu.make_async_remote_copy(
        src_ref=keys_values.at[side], dst_ref=keys_values.at[side],
        send_sem=kv_send, recv_sem=kv_recv,
        device_id={"row": 1 - side}, device_id_type=pl.DeviceIdType.MESH,
    )
    kv_copy.start()

    loads[14].wait()
    change = dot_nn(right_terms, mixer_terms)
    for row in range(rows):
        slab, place = row // slab_rows, row % slab_rows
        updated = pair[slab, place] + change[:, row * channels : (row + 1) * channels]
        new_pair[slab, place] = updated
        upper = rounded(updated)
        both = jnp.concatenate([upper, updated - upper], axis=1).astype(jnp.bfloat16)
        logits = dot_nt(bias_terms, both)
        differ = (chains != query_chain[slab, place]).astype(jnp.float32)
        bias[slab, place] = logits[:slots] + logits[slots:] + chain_column * differ


    for copy in q_copies:
        copy.wait()
    half = cols // 2
    query = jnp.concatenate(
        [parts_q[place].astype(jnp.float32) for place in range(half)], axis=1
    )
    gate = jax.nn.sigmoid(
        jnp.concatenate(
            [parts_q[place].astype(jnp.float32) for place in range(half, cols)], axis=1
        )
    )
    for place in range(cols):
        gates[place] = gate[place * own_rows : (place + 1) * own_rows]
    on_head = (
        iota((1, slots, width), 2) // head_width == iota((1, slots, width), 1)
    ).astype(jnp.float32)
    query_blocks = (
        (on_head * query[:, None, :])
        .reshape(rows * slots, width)
        .astype(jnp.bfloat16)
    )
    kv_copy.wait()
    scores = dot_nt(query_blocks, keys_values[0]) * (1.0 / math.sqrt(head_width)) + bias[
        ...
    ].reshape(rows * slots, keys)
    maxima = jnp.max(scores, axis=1, keepdims=True)
    exponent = jnp.exp(scores - maxima)
    totals = jnp.sum(exponent, axis=1, keepdims=True)
    summed = dot_nn(exponent.astype(jnp.bfloat16), keys_values[1]).reshape(rows, slots, width)
    summed = jnp.sum(on_head * summed, axis=1)
    on_lane = (iota((1, slots, LANES), 2) == iota((1, slots, LANES), 1)).astype(jnp.float32)

    def by_lane(column):
        return jnp.sum(on_lane * column.reshape(rows, slots, 1), axis=1)

    bundle = jnp.concatenate([summed, by_lane(maxima), by_lane(totals)], axis=1)
    for place in range(cols):
        packed[place] = bundle[place * own_rows : (place + 1) * own_rows]
    p_copies = [
        pltpu.make_async_remote_copy(
            src_ref=packed.at[peer], dst_ref=partial.at[me],
            send_sem=p_send.at[place], recv_sem=p_recv.at[place],
            device_id={"col": peer}, device_id_type=pl.DeviceIdType.MESH,
        )
        for place, peer in enumerate(peers)
    ]
    for copy in p_copies:
        copy.start()
    partial[me] = packed[me]
    gate_own = gates[me]
    spread_heads = (
        iota((2 * LANES, width), 1) // head_width == iota((2 * LANES, width), 0) % LANES
    ).astype(jnp.bfloat16)
    loads[15].wait()
    for copy in p_copies:
        copy.wait()

    maxima = [partial[place, :, width : width + LANES] for place in range(cols)]
    totals = [partial[place, :, width + LANES :] for place in range(cols)]
    peak = functools.reduce(jnp.maximum, maxima)
    scales = [jnp.exp(part - peak) for part in maxima]
    total = functools.reduce(jnp.add, [a * b for a, b in zip(totals, scales)])
    total = jnp.where(iota(total.shape, 1) < heads, total, 1.0)
    share = jnp.concatenate([scale / total for scale in scales], axis=0)
    upper = rounded(share)
    shares = dot_nn(
        jnp.concatenate([upper, share - upper], axis=1).astype(jnp.bfloat16), spread_heads
    )
    joint = functools.reduce(
        jnp.add,
        [
            shares[place * own_rows : (place + 1) * own_rows] * partial[place, :, :width]
            for place in range(cols)
        ],
    )
    attended = joint * gate_own
    attended = jnp.concatenate(
        [attended, jnp.zeros((rows - own_rows, width), jnp.float32)], axis=0
    ).astype(jnp.bfloat16)

    final[me] = rounded(dot_nn(attended, out_proj[...])[:own_rows])
    f_copies = [
        pltpu.make_async_remote_copy(
            src_ref=final.at[me], dst_ref=final.at[me],
            send_sem=f_send.at[place], recv_sem=f_recv.at[place],
            device_id={"col": peer}, device_id_type=pl.DeviceIdType.MESH,
        )
        for place, peer in enumerate(peers)
    ]
    for copy in f_copies:
        copy.start()
    for copy in f_copies:
        copy.wait()
    single_update[...] = (
        jnp.concatenate([final[place] for place in range(cols)], axis=0)
        .reshape(slabs, slab_rows, width)
        .astype(jnp.bfloat16)
    )


LANES = 128
OPERANDS = 16
PIECES = 4
VMEM_BYTES = 60 * 1024 * 1024


def hand_on(pair_in, update_in, pair_out, update_out, pair_sem, update_sem):
    slabs = pair_in.shape[0]
    copies = [
        pltpu.make_async_copy(pair_in.at[slab], pair_out.at[slab], pair_sem.at[slab])
        for slab in range(slabs)
    ] + [pltpu.make_async_copy(update_in, update_out, update_sem)]
    for copy in copies:
        copy.start()
    for copy in copies:
        copy.wait()


def fused(
    pair_block, query_single, key_single, query_chain, key_chain, query_mask, key_mask,
    timestep, time_table, norm_gain, left_proj, right_proj, outer_proj, bias_proj,
    chain_weight, query_proj, kv_proj, out_proj,
):
    cols = lax.axis_size("col")
    slabs, slab_rows, width = query_single.shape
    rows = slabs * slab_rows
    keys = key_single.shape[0]
    heads = chain_weight.shape[0]
    slots = -(-heads // 16) * 16
    own_rows = rows // cols
    operands = (
        time_table, query_single, query_mask, norm_gain.reshape(-1, LANES), query_proj.T,
        key_single, key_mask.reshape(1, -1), kv_proj, left_proj.T, right_proj.T, outer_proj,
        bias_proj.T, chain_weight.reshape(1, -1), key_chain.reshape(1, -1), pair_block, out_proj,
    )
    smem = pl.BlockSpec(memory_space=pltpu.SMEM)
    near = pl.BlockSpec(memory_space=pltpu.VMEM)
    far = pl.BlockSpec(memory_space=pltpu.HBM)
    dma = pltpu.SemaphoreType.DMA
    results = pl.pallas_call(
        fused_kernel,
        out_shape=(
            pltpu.VMEM(pair_block.shape, jnp.float32),
            pltpu.VMEM(query_single.shape, jnp.bfloat16),
        ),
        in_specs=[smem, smem] + [far] * len(operands),
        out_specs=(near, near),
        scratch_shapes=[pltpu.VMEM(operand.shape, operand.dtype) for operand in operands]
        + [
            pltpu.VMEM((cols, rows, query_proj.shape[1]), jnp.bfloat16),
            pltpu.VMEM((2, keys, width), jnp.bfloat16),
            pltpu.VMEM((slabs, slab_rows, slots, keys), jnp.float32),
            pltpu.VMEM((cols, own_rows, width + 2 * LANES), jnp.float32),
            pltpu.VMEM((cols, own_rows, width + 2 * LANES), jnp.float32),
            pltpu.VMEM((cols, own_rows, width), jnp.float32),
            pltpu.VMEM((cols, own_rows, width), jnp.float32),
            dma((len(operands), PIECES)),
            dma((cols - 1,)),
            dma((cols - 1,)),
            dma,
            dma,
            dma((cols - 1,)),
            dma((cols - 1,)),
            dma((cols - 1,)),
            dma((cols - 1,)),
        ],
        compiler_params=pltpu.CompilerParams(
            collective_id=0, has_side_effects=True, vmem_limit_bytes=VMEM_BYTES
        ),
    )(query_chain, timestep, *operands)
    return pl.pallas_call(
        hand_on,
        out_shape=tuple(jax.ShapeDtypeStruct(part.shape, part.dtype) for part in results),
        in_specs=[near, near],
        out_specs=(far, far),
        scratch_shapes=[dma((slabs,)), dma],
        compiler_params=pltpu.CompilerParams(vmem_limit_bytes=VMEM_BYTES // 60),
    )(*results)


def serve(*arrays):
    query_single, chain_weight, kv_proj = arrays[1], arrays[14], arrays[16]
    rows = query_single.shape[0] * query_single.shape[1]
    cols = lax.axis_size("col")
    fits = (
        rows % cols == 0
        and cols % 2 == 0
        and lax.axis_size("row") == 2
        and kv_proj.shape[1] == query_single.shape[2]
        and chain_weight.shape[0] <= LANES
        and query_single.shape[2] % LANES == 0
    )
    return fused(*arrays) if fits else on_device(*arrays)


def solution(mesh):
    return jax.shard_map(
        serve,
        mesh=mesh,
        in_specs=(
            P("grp", "row", "col", None),
            P("grp", "row", None),
            P(("grp", "col"), None),
            P("grp", "row"),
            P(("grp", "col")),
            P("grp", "row"),
            P(("grp", "col")),
            P("grp"),
            P(),
            P(),
            P(),
            P(),
            P(),
            P(),
            P(),
            P(None, "col"),
            P(None, "row"),
            P(),
        ),
        out_specs=(P("grp", "row", "col", None), P("grp", "row", None)),
        check_vma=False,
    )
```
